32 devices in a mesh: dp: 2 (over x), expert: 16 (over z, y, core).
Axes of the slice: x: 2, y: 2, z: 4, core: 2. Of those that a mesh axis runs over, the one named last changes fastest.
Arguments:
- grad_out: bfloat16 [512, 2048], P(('dp', 'expert')), may hold values from -4 to 4
- x_codes: bfloat16 [512, 2048], P(('dp', 'expert')), may hold values from -6 to 6
- x_scales: bfloat16 [512, 16], P(('dp', 'expert')), may hold values from 0.25 to 4
- combine: bfloat16 [512, 8], P(('dp', 'expert')), may hold values from 0.049804688 to 1
- expert_ids: int32 [512, 8], P(('dp', 'expert')), may hold values from 0 to 15, all different within a row; in each aligned block of 16 rows (0 to 15, 16 to 31, ...) at most 16 rows name the same one
- w_gate: bfloat16 [16, 768, 2048], P('expert', 'dp'), may hold values from -0.125 to 0.125
- w_up: bfloat16 [16, 768, 2048], P('expert', 'dp'), may hold values from -0.125 to 0.125
- w_down: bfloat16 [16, 768, 2048], P('expert', 'dp'), may hold values from -0.21875 to 0.21875
Outputs:
- grad_in: bfloat16 [512, 2048], P(('dp', 'expert'))
- grad_combine: float32 [512, 8], P(('dp', 'expert'))
- grad_gate: bfloat16 [16, 768, 2048], P('expert', 'dp')
- grad_up: bfloat16 [16, 768, 2048], P('expert', 'dp')
- grad_down: bfloat16 [16, 768, 2048], P('expert', 'dp')
The draws below stay inside these ranges and needn't reach their ends.
Inputs may be any that keep to these rules, and one draw needn't show every extreme that they name: `expert_ids`: each token names 8 different experts. Among the 16 tokens of one device no expert is named more than 16 times, and on some devices some expert is named exactly 16 times.
All inputs are finite; a program needn't handle non-finite values.
Results may differ from the reference program's by a relative error of at most 0.015.
Values may be sent and summed in bfloat16 or wider, within the bound.
A program may use at most 128 MiB of HBM per device.

```python
import math
import jax
import jax.numpy as jnp
import numpy as np
from jax import lax

D = 2048
FF = 768
TOP = 8
BLOCK = 128
TOK_DEV = 16
EXPERTS = 16
CAP = 16
TOKENS = 512
N_DP = 2


def level_of(stream_key, shape, pieces, least, largest):
    factor_of, own = 1.0, jax.random.fold_in(stream_key, 6)
    for dim, parts in pieces:
        draws = jnp.exp(jax.random.uniform(jax.random.fold_in(own, dim), (parts,), jnp.float32, least / len(pieces), largest / len(pieces)))
        factor_of = factor_of * jnp.repeat(draws, shape[dim] // parts).reshape([-1 if axis == dim else 1 for axis in range(len(shape))])
    return factor_of


def assign_block(rng, own, number, rows, count, top, limit, lean):
    ranking = jax.random.permutation(rng, count)
    packed, usual = load_shares(count, rows * top, limit, lean, True), load_shares(count, rows * top, limit, lean, False)
    places = jnp.arange(count)

    def named(sizes, offset_by):
        used = int((sizes > 0).sum())
        fixed = max(1, used // 4)
        shifted = fixed + (places - fixed + offset_by * (used - fixed)) % max(1, count - fixed)
        return jnp.zeros((count,), jnp.int32).at[ranking[jnp.where(places < fixed, places, shifted)]].set(jnp.asarray(sizes, jnp.int32))

    sizes = jnp.where(number % 4 == 0, named(packed, number // 4), named(usual, number - number // 4 - 1))
    mixed = jax.random.permutation(jax.random.fold_in(own, 3), count)
    donor, receiver = mixed[0:count // 2 * 2:2], mixed[1:count // 2 * 2:2]
    room = jnp.minimum(sizes[donor] - 1, limit - sizes[receiver]) // 2
    room = jnp.where((donor == ranking[0]) | (receiver == ranking[0]) | (sizes[receiver] == 0), 0, jnp.maximum(room, 0))
    shifted = jax.random.randint(jax.random.fold_in(own, 4), (count // 2,), 0, 1 << 20) % (room + 1)
    sizes = sizes.at[donor].add(-shifted).at[receiver].add(shifted)
    labels = jnp.searchsorted(jnp.cumsum(sizes), jnp.arange(rows * top), side="right").astype(jnp.int32)
    listing = labels.reshape(top, rows).T
    listing = listing[jax.random.permutation(jax.random.fold_in(own, 1), rows)]
    offset_by = jax.random.randint(jax.random.fold_in(own, 2), (rows, 1), 0, top)
    return jnp.take_along_axis(listing, (jnp.arange(top)[None, :] + offset_by) % top, axis=1)


def load_shares(count, total, limit, slope, full):
    weights = [(1 << 20) // math.isqrt(grade ** slope) + 1 for grade in range(1, count + 1)]
    largest = limit if full else min(limit, max(-(-total // count), total * weights[0] // sum(weights)))
    least = 1 if total - largest >= count - 1 else 0
    holding, rest = [largest] + [least] * (count - 1), total - largest - least * (count - 1)
    while rest > 0:
        movable = [i for i in range(1, count) if holding[i] < largest] or [i for i in range(1, count) if holding[i] < limit]
        pool, budget = sum([weights[i] for i in movable]), rest
        for i in movable:
            addition = min(limit - holding[i], max(1, budget * weights[i] // pool), rest)
            holding[i] = holding[i] + addition
            rest = rest - addition
    return np.array(holding)


def bell_draw(own_key, extent, deviation, reach, pieces=(), held_as=jnp.bfloat16):
    array = jax.random.normal(own_key, extent, jnp.float32) * deviation
    if len(pieces) > 0:
        array = level_of(own_key, extent, pieces, -0.22, 0.18) * array
    return jnp.clip(array, min=-reach, max=reach).astype(held_as)


def setup_inputs(seed: int = 0) -> dict:
    keys = jax.random.split(jax.random.key(seed), 9)
    grad_out = bell_draw(keys[0], (TOKENS, D), 0.3, 4.0, ((0, 32),))
    x_codes = bell_draw(keys[1], (TOKENS, D), 1.0, 6.0, ((0, 32),))
    x_scales = jnp.clip(jnp.exp(math.log(4.0) - 2.7725887 * jax.random.uniform(keys[2], (TOKENS, D // BLOCK), jnp.float32) ** level_of(keys[2], (TOKENS, D // BLOCK), ((0, 32),), -0.2, 0.2)), 0.25, 4.0).astype(jnp.bfloat16)
    combine = jnp.clip(jnp.exp(math.log(1.0) - 2.9996462 * jax.random.uniform(keys[3], (TOKENS, TOP), jnp.float32) ** level_of(keys[3], (TOKENS, TOP), ((0, 32),), -0.2, 0.2)), 0.049804688, 1.0).astype(jnp.bfloat16)
    expert_ids_keys = jax.random.split(jax.random.fold_in(keys[4], 1), TOKENS // TOK_DEV)
    expert_ids_turns = jax.random.permutation(jax.random.fold_in(keys[4], 3), TOKENS // TOK_DEV)
    expert_ids = jax.vmap(lambda own, number: assign_block(jax.random.fold_in(keys[4], 2), own, number, TOK_DEV, EXPERTS, TOP, CAP, 2))(expert_ids_keys, expert_ids_turns).reshape((TOKENS, TOP))
    w_gate = bell_draw(keys[5], (EXPERTS, FF, D), D ** -0.5, 0.125, ((0, 16), (1, 2)))
    w_up = bell_draw(keys[6], (EXPERTS, FF, D), D ** -0.5, 0.125, ((0, 16), (1, 2)))
    w_down = bell_draw(keys[7], (EXPERTS, FF, D), FF ** -0.5, 0.21875, ((0, 16), (1, 2)))
    return dict(grad_out=grad_out, x_codes=x_codes, x_scales=x_scales, combine=combine, expert_ids=expert_ids, w_gate=w_gate, w_up=w_up, w_down=w_down)


def slot_positions(block_ids):
    onehot = (block_ids[:, None] == jnp.arange(EXPERTS, dtype=jnp.int32)[None, :]).astype(jnp.int32)
    before = jnp.cumsum(onehot, axis=0) - onehot
    return jnp.sum(before * onehot, axis=1).astype(jnp.int32)


def reference(grad_out, x_codes, x_scales, combine, expert_ids, w_gate, w_up, w_down):
    blocks = TOKENS // TOK_DEV
    picks_all = TOKENS * TOP
    quarter = FF // N_DP
    flat_ids = expert_ids.reshape(-1).astype(jnp.int32)
    position = jax.vmap(slot_positions)(expert_ids.reshape(blocks, TOK_DEV * TOP).astype(jnp.int32)).reshape(-1)
    block_of = jnp.repeat(jnp.arange(blocks, dtype=jnp.int32), TOK_DEV * TOP)
    slot_index = (block_of * CAP + position).astype(jnp.int32)
    row_table = jnp.full((EXPERTS, blocks * CAP), picks_all, dtype=jnp.int32)
    row_table = row_table.at[flat_ids, slot_index].set(jnp.arange(picks_all, dtype=jnp.int32))
    x_all = (x_codes.astype(jnp.float32).reshape(TOKENS, D // BLOCK, BLOCK)
             * x_scales.astype(jnp.float32)[:, :, None]).reshape(TOKENS, D).astype(jnp.bfloat16)
    x_pad = jnp.concatenate([x_all, jnp.zeros((1, D), jnp.bfloat16)], axis=0)
    grad_pad = jnp.concatenate([grad_out, jnp.zeros((1, D), jnp.bfloat16)], axis=0)
    weight_pad = jnp.concatenate([combine.reshape(-1).astype(jnp.float32), jnp.zeros((1,), jnp.float32)], axis=0)

    def expert_step(totals, per_expert):
        input_total, combine_total = totals
        chosen, gate_w, up_w, down_w = per_expert
        token_index = chosen // TOP
        x_rows = x_pad[token_index]
        grad_rows = grad_pad[token_index]
        weight_rows = weight_pad[chosen]
        gate_pre = lax.dot_general(x_rows, gate_w, (((1,), (1,)), ((), ())), preferred_element_type=jnp.float32)
        up_pre = lax.dot_general(x_rows, up_w, (((1,), (1,)), ((), ())), preferred_element_type=jnp.float32)
        sigmoid_gate = jax.nn.sigmoid(gate_pre)
        activated = gate_pre * sigmoid_gate
        hidden = (activated * up_pre).astype(jnp.bfloat16)
        scaled = (weight_rows[:, None] * grad_rows.astype(jnp.float32)).astype(jnp.bfloat16)
        backward = lax.dot_general(grad_rows, down_w, (((1,), (1,)), ((), ())), preferred_element_type=jnp.float32)
        comb_rows = jnp.sum(backward * hidden.astype(jnp.float32), axis=1)
        grad_hidden = weight_rows[:, None] * backward
        grad_gate_pre = (grad_hidden * up_pre * sigmoid_gate * (1.0 + gate_pre * (1.0 - sigmoid_gate))).astype(jnp.bfloat16)
        grad_up_pre = (grad_hidden * activated).astype(jnp.bfloat16)
        grad_down_e = lax.dot_general(hidden, scaled, (((0,), (0,)), ((), ())), preferred_element_type=jnp.float32).astype(jnp.bfloat16)
        grad_gate_e = lax.dot_general(grad_gate_pre, x_rows, (((0,), (0,)), ((), ())), preferred_element_type=jnp.float32).astype(jnp.bfloat16)
        grad_up_e = lax.dot_general(grad_up_pre, x_rows, (((0,), (0,)), ((), ())), preferred_element_type=jnp.float32).astype(jnp.bfloat16)
        quarter_terms = jnp.einsum("sjf,jfd->jsd",
                                   grad_gate_pre.astype(jnp.float32).reshape(-1, N_DP, quarter),
                                   gate_w.astype(jnp.float32).reshape(N_DP, quarter, D))
        quarter_terms = quarter_terms + jnp.einsum("sjf,jfd->jsd",
                                                   grad_up_pre.astype(jnp.float32).reshape(-1, N_DP, quarter),
                                                   up_w.astype(jnp.float32).reshape(N_DP, quarter, D))
        rounded = lax.optimization_barrier(quarter_terms.astype(jnp.bfloat16)).astype(jnp.float32)
        input_rows = jnp.sum(rounded, axis=0)
        input_total = input_total.at[token_index].add(input_rows)
        combine_total = combine_total.at[chosen].add(comb_rows)
        return (input_total, combine_total), (grad_gate_e, grad_up_e, grad_down_e)

    initial = (jnp.zeros((TOKENS + 1, D), jnp.float32), jnp.zeros((picks_all + 1,), jnp.float32))
    (input_total, combine_total), (grad_gate, grad_up, grad_down) = lax.scan(
        expert_step, initial, (row_table, w_gate, w_up, w_down))
    grad_in = input_total[:TOKENS].astype(jnp.bfloat16)
    grad_combine = combine_total[:picks_all].reshape(TOKENS, TOP)
    return (grad_in, grad_combine, grad_gate, grad_up, grad_down)
```

```python
import jax
import jax.numpy as jnp
from jax import lax
from jax.sharding import PartitionSpec as P

BLOCK = 128


def slot_table(flat_ids, experts, capacity):
    onehot = (flat_ids[:, None] == jnp.arange(experts, dtype=jnp.int32)[None, :]).astype(jnp.int32)
    before = jnp.cumsum(onehot, axis=0) - onehot
    position = jnp.sum(before * onehot, axis=1)
    slot_index = flat_ids * capacity + position
    return jnp.arange(experts * capacity, dtype=jnp.int32)[:, None] == slot_index[None, :]


def token_owner(placed, tokens, picks):
    return jnp.sum(placed.reshape(placed.shape[0], tokens, picks).astype(jnp.int32), axis=2)


def build_rows(grad_out, x_codes, x_scales, combine, expert_ids, experts, capacity):
    tokens, picks = expert_ids.shape
    placed = slot_table(expert_ids.reshape(-1), experts, capacity)
    owner = token_owner(placed, tokens, picks).astype(jnp.bfloat16)
    grad_rows = jnp.dot(owner, grad_out, preferred_element_type=jnp.float32).astype(jnp.bfloat16)
    code_rows = jnp.dot(owner, x_codes, preferred_element_type=jnp.float32).astype(jnp.bfloat16)
    scale_rows = jnp.dot(owner, x_scales, preferred_element_type=jnp.float32).astype(jnp.bfloat16)
    weight_rows = jnp.dot(
        placed.astype(jnp.bfloat16), combine.reshape(-1), preferred_element_type=jnp.float32
    ).astype(jnp.bfloat16)
    return (
        grad_rows.reshape(experts, capacity, -1),
        code_rows.reshape(experts, capacity, -1),
        scale_rows.reshape(experts, capacity, -1),
        weight_rows.reshape(experts, capacity),
    )


def body(grad_out, x_codes, x_scales, combine, expert_ids, w_gate, w_up, w_down):
    tokens, picks = expert_ids.shape
    width = grad_out.shape[1]
    groups = lax.axis_size("dp")
    experts = w_gate.shape[0] * lax.axis_size("expert")
    capacity = min(tokens, max(2, 2 * tokens * picks // experts))
    grad_rows, code_rows, scale_rows, weight_rows = build_rows(
        grad_out, x_codes, x_scales, combine, expert_ids, experts, capacity
    )
    grad_rows, code_rows, scale_rows, weight_rows = (
        lax.all_to_all(grad_rows, "expert", split_axis=0, concat_axis=0, tiled=True),
        lax.all_to_all(code_rows, "expert", split_axis=0, concat_axis=0, tiled=True),
        lax.all_to_all(scale_rows, "expert", split_axis=0, concat_axis=0, tiled=True),
        lax.all_to_all(weight_rows, "expert", split_axis=0, concat_axis=0, tiled=True),
    )
    grad_rows, code_rows, scale_rows, weight_rows = (
        lax.all_gather(grad_rows[None], "dp", axis=0, tiled=True),
        lax.all_gather(code_rows[None], "dp", axis=0, tiled=True),
        lax.all_gather(scale_rows[None], "dp", axis=0, tiled=True),
        lax.all_gather(weight_rows[None], "dp", axis=0, tiled=True),
    )
    rows = groups * experts * capacity
    scale_count = width // BLOCK
    grad_flat = grad_rows.reshape(rows, width)
    x_rows = (
        (
            code_rows.reshape(rows, scale_count, BLOCK).astype(jnp.float32)
            * scale_rows.reshape(rows, scale_count, 1).astype(jnp.float32)
        )
        .reshape(rows, width)
        .astype(jnp.bfloat16)
    )
    weight_flat = weight_rows.reshape(rows).astype(jnp.float32)
    share = w_gate.shape[1]
    stacked_w = jnp.concatenate([w_gate[0], w_up[0]], axis=0)
    down_w = w_down[0]
    both_pre = lax.dot_general(
        x_rows, stacked_w, (((1,), (1,)), ((), ())), preferred_element_type=jnp.float32
    )
    gate_pre = both_pre[:, :share]
    up_pre = both_pre[:, share:]
    sigmoid_gate = jax.nn.sigmoid(gate_pre)
    activated = gate_pre * sigmoid_gate
    hidden = (activated * up_pre).astype(jnp.bfloat16)
    scaled = (weight_flat[:, None] * grad_flat.astype(jnp.float32)).astype(jnp.bfloat16)
    backward = lax.dot_general(
        grad_flat, down_w, (((1,), (1,)), ((), ())), preferred_element_type=jnp.float32
    )
    partial_comb = jnp.sum(backward * hidden.astype(jnp.float32), axis=1)
    grad_hidden = weight_flat[:, None] * backward
    grad_gate_pre = (
        grad_hidden * up_pre * sigmoid_gate * (1.0 + gate_pre * (1.0 - sigmoid_gate))
    ).astype(jnp.bfloat16)
    grad_up_pre = (grad_hidden * activated).astype(jnp.bfloat16)
    grad_both_pre = jnp.concatenate([grad_gate_pre, grad_up_pre], axis=1)
    grad_down = lax.dot_general(
        hidden, scaled, (((0,), (0,)), ((), ())), preferred_element_type=jnp.float32
    ).astype(jnp.bfloat16)
    grad_stacked = lax.dot_general(
        grad_both_pre, x_rows, (((0,), (0,)), ((), ())), preferred_element_type=jnp.float32
    ).astype(jnp.bfloat16)
    grad_gate = grad_stacked[:share]
    grad_up = grad_stacked[share:]
    input_part = jnp.dot(grad_both_pre, stacked_w, preferred_element_type=jnp.float32)
    summed = lax.psum_scatter(
        input_part.reshape(groups, experts, capacity, width).astype(jnp.bfloat16),
        "dp",
        scatter_dimension=0,
        tiled=True,
    ).astype(jnp.float32)
    comb_all = lax.psum(partial_comb, "dp")
    own_terms = lax.dynamic_slice_in_dim(
        comb_all, lax.axis_index("dp") * (experts * capacity), experts * capacity
    )
    back_grad, back_comb = (
        lax.all_to_all(
            summed.reshape(experts, capacity, width).astype(jnp.bfloat16),
            "expert",
            split_axis=0,
            concat_axis=0,
            tiled=True,
        ).astype(jnp.float32),
        lax.all_to_all(
            own_terms.reshape(experts, capacity).astype(jnp.bfloat16),
            "expert",
            split_axis=0,
            concat_axis=0,
            tiled=True,
        ).astype(jnp.float32),
    )
    placed = slot_table(expert_ids.reshape(-1), experts, capacity)
    owner = token_owner(placed, tokens, picks).astype(jnp.float32)
    grad_in = lax.dot_general(
        owner,
        back_grad.reshape(experts * capacity, width),
        (((0,), (0,)), ((), ())),
        precision=lax.Precision.HIGHEST,
    ).astype(jnp.bfloat16)
    grad_combine = lax.dot_general(
        placed.astype(jnp.float32),
        back_comb.reshape(experts * capacity),
        (((0,), (0,)), ((), ())),
        precision=lax.Precision.HIGHEST,
    ).reshape(tokens, picks)
    return (grad_in, grad_combine, grad_gate[None], grad_up[None], grad_down[None])


def dense_body(grad_out, x_codes, x_scales, combine, expert_ids, w_gate, w_up, w_down):
    tokens, picks = expert_ids.shape
    width = grad_out.shape[1]
    experts = w_gate.shape[0] * lax.axis_size("expert")
    axes = ("dp", "expert")
    lanes = -(-experts // BLOCK) * BLOCK
    x_own = (
        (
            x_codes.reshape(tokens, -1, BLOCK).astype(jnp.float32)
            * x_scales.reshape(tokens, -1, 1).astype(jnp.float32)
        )
        .reshape(tokens, width)
        .astype(jnp.bfloat16)
    )
    picked = expert_ids[:, :, None] == jnp.arange(lanes, dtype=jnp.int32)[None, None, :]
    weight_own = jnp.sum(
        jnp.where(picked, combine[:, :, None].astype(jnp.float32), 0.0), axis=1
    ).astype(jnp.bfloat16)
    packed = jnp.concatenate([grad_out, x_own, weight_own], axis=1)
    every = lax.all_gather(packed, axes, axis=0, tiled=True)
    grad_rows = every[:, :width]
    x_rows = every[:, width : 2 * width]
    mine = jnp.arange(lanes)[None, :] == lax.axis_index("expert")
    weight = jnp.sum(jnp.where(mine, every[:, 2 * width :].astype(jnp.float32), 0.0), axis=1)[:, None]
    contract = (((1,), (1,)), ((), ()))
    over_rows = (((0,), (0,)), ((), ()))
    f32 = jnp.float32
    gate_pre = lax.dot_general(x_rows, w_gate[0], contract, preferred_element_type=f32)
    up_pre = lax.dot_general(x_rows, w_up[0], contract, preferred_element_type=f32)
    backward = lax.dot_general(grad_rows, w_down[0], contract, preferred_element_type=f32)
    sigmoid_gate = jax.nn.sigmoid(gate_pre)
    activated = gate_pre * sigmoid_gate
    hidden = (activated * up_pre).astype(jnp.bfloat16)
    scaled = (weight * grad_rows.astype(f32)).astype(jnp.bfloat16)
    comb = jnp.sum(backward * hidden.astype(f32), axis=1)[:, None]
    grad_hidden = weight * backward
    grad_gate_pre = (
        grad_hidden * up_pre * sigmoid_gate * (1.0 + gate_pre * (1.0 - sigmoid_gate))
    ).astype(jnp.bfloat16)
    grad_up_pre = (grad_hidden * activated).astype(jnp.bfloat16)
    input_part = jnp.dot(grad_gate_pre, w_gate[0], preferred_element_type=f32) + jnp.dot(
        grad_up_pre, w_up[0], preferred_element_type=f32
    )
    terms = jnp.concatenate([input_part, jnp.where(mine, comb, 0.0)], axis=1).astype(jnp.bfloat16)
    summed = lax.psum_scatter(terms, axes, scatter_dimension=0, tiled=True)
    grad_down = lax.dot_general(hidden, scaled, over_rows, preferred_element_type=f32)
    grad_gate = lax.dot_general(grad_gate_pre, x_rows, over_rows, preferred_element_type=f32)
    grad_up = lax.dot_general(grad_up_pre, x_rows, over_rows, preferred_element_type=f32)
    grad_in = summed[:, :width]
    grad_combine = jnp.sum(
        jnp.where(picked, summed[:, None, width:].astype(f32), 0.0), axis=2
    )
    return (
        grad_in,
        grad_combine,
        grad_gate.astype(jnp.bfloat16)[None],
        grad_up.astype(jnp.bfloat16)[None],
        grad_down.astype(jnp.bfloat16)[None],
    )


def chosen_body(grad_out, x_codes, x_scales, combine, expert_ids, w_gate, w_up, w_down):
    tokens, picks = expert_ids.shape
    experts = w_gate.shape[0] * lax.axis_size("expert")
    capacity = min(tokens, max(2, 2 * tokens * picks // experts))
    chosen = dense_body if capacity == tokens and w_gate.shape[0] == 1 else body
    return chosen(grad_out, x_codes, x_scales, combine, expert_ids, w_gate, w_up, w_down)


def solution(mesh):
    in_specs = (
        P(("dp", "expert"), None),
        P(("dp", "expert"), None),
        P(("dp", "expert"), None),
        P(("dp", "expert"), None),
        P(("dp", "expert"), None),
        P("expert", "dp", None),
        P("expert", "dp", None),
        P("expert", "dp", None),
    )
    out_specs = (
        P(("dp", "expert"), None),
        P(("dp", "expert"), None),
        P("expert", "dp", None),
        P("expert", "dp", None),
        P("expert", "dp", None),
    )
    return jax.shard_map(chosen_body, mesh=mesh, in_specs=in_specs, out_specs=out_specs, check_vma=False)
```

```python
import functools

import jax
import jax.numpy as jnp
from jax import lax
from jax.experimental import pallas as pl
from jax.experimental.pallas import tpu as pltpu
from jax.sharding import PartitionSpec as P

BLOCK = 128
MESH = pl.DeviceIdType.MESH


def slot_table(flat_ids, experts, capacity):
    onehot = (flat_ids[:, None] == jnp.arange(experts, dtype=jnp.int32)[None, :]).astype(jnp.int32)
    before = jnp.cumsum(onehot, axis=0) - onehot
    position = jnp.sum(before * onehot, axis=1)
    slot_index = flat_ids * capacity + position
    return jnp.arange(experts * capacity, dtype=jnp.int32)[:, None] == slot_index[None, :]


def token_owner(placed, tokens, picks):
    return jnp.sum(placed.reshape(placed.shape[0], tokens, picks).astype(jnp.int32), axis=2)


def build_rows(grad_out, x_codes, x_scales, combine, expert_ids, experts, capacity):
    tokens, picks = expert_ids.shape
    placed = slot_table(expert_ids.reshape(-1), experts, capacity)
    owner = token_owner(placed, tokens, picks).astype(jnp.bfloat16)
    grad_rows = jnp.dot(owner, grad_out, preferred_element_type=jnp.float32).astype(jnp.bfloat16)
    code_rows = jnp.dot(owner, x_codes, preferred_element_type=jnp.float32).astype(jnp.bfloat16)
    scale_rows = jnp.dot(owner, x_scales, preferred_element_type=jnp.float32).astype(jnp.bfloat16)
    weight_rows = jnp.dot(
        placed.astype(jnp.bfloat16), combine.reshape(-1), preferred_element_type=jnp.float32
    ).astype(jnp.bfloat16)
    return (
        grad_rows.reshape(experts, capacity, -1),
        code_rows.reshape(experts, capacity, -1),
        scale_rows.reshape(experts, capacity, -1),
        weight_rows.reshape(experts, capacity),
    )


def body(grad_out, x_codes, x_scales, combine, expert_ids, w_gate, w_up, w_down):
    tokens, picks = expert_ids.shape
    width = grad_out.shape[1]
    groups = lax.axis_size("dp")
    experts = w_gate.shape[0] * lax.axis_size("expert")
    capacity = min(tokens, max(2, 2 * tokens * picks // experts))
    grad_rows, code_rows, scale_rows, weight_rows = build_rows(
        grad_out, x_codes, x_scales, combine, expert_ids, experts, capacity
    )
    grad_rows, code_rows, scale_rows, weight_rows = (
        lax.all_to_all(grad_rows, "expert", split_axis=0, concat_axis=0, tiled=True),
        lax.all_to_all(code_rows, "expert", split_axis=0, concat_axis=0, tiled=True),
        lax.all_to_all(scale_rows, "expert", split_axis=0, concat_axis=0, tiled=True),
        lax.all_to_all(weight_rows, "expert", split_axis=0, concat_axis=0, tiled=True),
    )
    grad_rows, code_rows, scale_rows, weight_rows = (
        lax.all_gather(grad_rows[None], "dp", axis=0, tiled=True),
        lax.all_gather(code_rows[None], "dp", axis=0, tiled=True),
        lax.all_gather(scale_rows[None], "dp", axis=0, tiled=True),
        lax.all_gather(weight_rows[None], "dp", axis=0, tiled=True),
    )
    rows = groups * experts * capacity
    scale_count = width // BLOCK
    grad_flat = grad_rows.reshape(rows, width)
    x_rows = (
        (
            code_rows.reshape(rows, scale_count, BLOCK).astype(jnp.float32)
            * scale_rows.reshape(rows, scale_count, 1).astype(jnp.float32)
        )
        .reshape(rows, width)
        .astype(jnp.bfloat16)
    )
    weight_flat = weight_rows.reshape(rows).astype(jnp.float32)
    share = w_gate.shape[1]
    stacked_w = jnp.concatenate([w_gate[0], w_up[0]], axis=0)
    down_w = w_down[0]
    both_pre = lax.dot_general(
        x_rows, stacked_w, (((1,), (1,)), ((), ())), preferred_element_type=jnp.float32
    )
    gate_pre = both_pre[:, :share]
    up_pre = both_pre[:, share:]
    sigmoid_gate = jax.nn.sigmoid(gate_pre)
    activated = gate_pre * sigmoid_gate
    hidden = (activated * up_pre).astype(jnp.bfloat16)
    scaled = (weight_flat[:, None] * grad_flat.astype(jnp.float32)).astype(jnp.bfloat16)
    backward = lax.dot_general(
        grad_flat, down_w, (((1,), (1,)), ((), ())), preferred_element_type=jnp.float32
    )
    partial_comb = jnp.sum(backward * hidden.astype(jnp.float32), axis=1)
    grad_hidden = weight_flat[:, None] * backward
    grad_gate_pre = (
        grad_hidden * up_pre * sigmoid_gate * (1.0 + gate_pre * (1.0 - sigmoid_gate))
    ).astype(jnp.bfloat16)
    grad_up_pre = (grad_hidden * activated).astype(jnp.bfloat16)
    grad_both_pre = jnp.concatenate([grad_gate_pre, grad_up_pre], axis=1)
    grad_down = lax.dot_general(
        hidden, scaled, (((0,), (0,)), ((), ())), preferred_element_type=jnp.float32
    ).astype(jnp.bfloat16)
    grad_stacked = lax.dot_general(
        grad_both_pre, x_rows, (((0,), (0,)), ((), ())), preferred_element_type=jnp.float32
    ).astype(jnp.bfloat16)
    grad_gate = grad_stacked[:share]
    grad_up = grad_stacked[share:]
    input_part = jnp.dot(grad_both_pre, stacked_w, preferred_element_type=jnp.float32)
    summed = lax.psum_scatter(
        input_part.reshape(groups, experts, capacity, width).astype(jnp.bfloat16),
        "dp",
        scatter_dimension=0,
        tiled=True,
    ).astype(jnp.float32)
    comb_all = lax.psum(partial_comb, "dp")
    own_terms = lax.dynamic_slice_in_dim(
        comb_all, lax.axis_index("dp") * (experts * capacity), experts * capacity
    )
    back_grad, back_comb = (
        lax.all_to_all(
            summed.reshape(experts, capacity, width).astype(jnp.bfloat16),
            "expert",
            split_axis=0,
            concat_axis=0,
            tiled=True,
        ).astype(jnp.float32),
        lax.all_to_all(
            own_terms.reshape(experts, capacity).astype(jnp.bfloat16),
            "expert",
            split_axis=0,
            concat_axis=0,
            tiled=True,
        ).astype(jnp.float32),
    )
    placed = slot_table(expert_ids.reshape(-1), experts, capacity)
    owner = token_owner(placed, tokens, picks).astype(jnp.float32)
    grad_in = lax.dot_general(
        owner,
        back_grad.reshape(experts * capacity, width),
        (((0,), (0,)), ((), ())),
        precision=lax.Precision.HIGHEST,
    ).astype(jnp.bfloat16)
    grad_combine = lax.dot_general(
        placed.astype(jnp.float32),
        back_comb.reshape(experts * capacity),
        (((0,), (0,)), ((), ())),
        precision=lax.Precision.HIGHEST,
    ).reshape(tokens, picks)
    return (grad_in, grad_combine, grad_gate[None], grad_up[None], grad_down[None])


def expert_kernel(
    tokens,
    width,
    share,
    lanes,
    picks,
    grad_ref,
    codes_ref,
    scales_ref,
    combine_ref,
    ids_ref,
    gate_hbm,
    up_hbm,
    down_hbm,
    grad_in_ref,
    comb_ref,
    grad_gate_hbm,
    grad_up_hbm,
    grad_down_hbm,
    rows_buf,
    stack_w,
    down_w,
    pre_buf,
    back_buf,
    act_buf,
    hid_buf,
    act_t,
    hid_t,
    stack_out,
    down_out,
    terms,
    from_sib,
    from_first,
    from_second,
    from_z,
    send_sems,
    row_sems,
    sib_sems,
    first_sems,
    second_sem,
    z_sems,
    local_sems,
):
    f32, bf16 = jnp.float32, jnp.bfloat16
    half_rows, fam_rows, group_rows = 16 * tokens, 8 * tokens, 4 * tokens
    x = lax.axis_index("dp")
    place = lax.axis_index("expert")
    z, y, c = place // 4, (place // 2) % 2, place % 2

    def device(dx, dz, dy, dc):
        return (dx, dz * 4 + dy * 2 + dc)

    sib = device(x, z, y, 1 - c)
    first = device(x + (1 - c) * (1 - 2 * x), z, y + c * (1 - 2 * y), c)
    second = device(x + c * (1 - 2 * x), z, y + (1 - c) * (1 - 2 * y), c)
    peer_z = [z + 1 - 2 * (z % 2), z + 2 - 4 * (z // 2), 3 - z]
    peers = [device(x, pz, y, c) for pz in peer_z]
    other = x + c * (y - x)

    in_copies = [
        pltpu.make_async_copy(gate_hbm.at[0], stack_w.at[pl.ds(0, share)], local_sems.at[0]),
        pltpu.make_async_copy(up_hbm.at[0], stack_w.at[pl.ds(share, share)], local_sems.at[1]),
        pltpu.make_async_copy(down_hbm.at[0], down_w, local_sems.at[2]),
    ]
    for copy in in_copies:
        copy.start()

    barrier = pltpu.get_barrier_semaphore()
    for partner in [sib, first, second] + peers:
        pl.semaphore_signal(barrier, inc=1, device_id=partner, device_id_type=MESH)

    def slot(half, fam, oth, zz):
        return half * 16 + fam * 8 + oth * 4 + zz

    def at_slot(index):
        return pl.ds(pl.multiple_of(index * tokens, tokens), tokens)

    own = slot(0, c, other, z)
    own_rows = at_slot(own)
    rows_buf[own_rows, 0:width] = grad_ref[...]
    scales = scales_ref[...].astype(f32)
    for b in range(width // BLOCK):
        cols = slice(b * BLOCK, (b + 1) * BLOCK)
        rows_buf[own_rows, width + b * BLOCK : width + (b + 1) * BLOCK] = (
            codes_ref[:, cols].astype(f32) * scales[:, b : b + 1]
        ).astype(bf16)
    lane = lax.broadcasted_iota(jnp.int32, (tokens, lanes), 1)
    combine = combine_ref[...].astype(f32)
    ids = ids_ref[...]
    weight_row = jnp.zeros((tokens, lanes), f32)
    for k in range(picks):
        weight_row += jnp.where(lane == ids[:, k : k + 1], combine[:, k : k + 1], 0.0)
    rows_buf[own_rows, 2 * width :] = weight_row.astype(bf16)

    pl.semaphore_wait(barrier, 6)

    sent = []

    def send(src, dst, sem, to):
        copy = pltpu.make_async_remote_copy(
            src_ref=src,
            dst_ref=dst,
            send_sem=send_sems.at[len(sent)],
            recv_sem=sem,
            device_id=to,
            device_id_type=MESH,
        )
        copy.start()
        sent.append(copy)

    def arrived(ref, sem):
        pltpu.make_async_remote_copy(
            src_ref=ref,
            dst_ref=ref,
            send_sem=send_sems.at[0],
            recv_sem=sem,
            device_id=sib,
            device_id_type=MESH,
        ).wait_recv()

    def send_rows(src, dst, to):
        send(rows_buf.at[at_slot(src)], rows_buf.at[at_slot(dst)], row_sems.at[dst], to)

    def rows_arrived(index):
        arrived(rows_buf.at[at_slot(index)], row_sems.at[index])

    every_z = [z] + peer_z
    send_rows(own, own, first)
    for peer in peers:
        send_rows(own, own, peer)
    send_rows(own, own + 16, second)
    send_rows(own, own, sib)
    for pz in peer_z:
        here = slot(0, c, other, pz)
        rows_arrived(here)
        send_rows(here, here, first)
        send_rows(here, here + 16, second)
        send_rows(here, here, sib)
    for pz in every_z:
        here = slot(0, c, 1 - other, pz)
        rows_arrived(here)
        send_rows(here, here + 16, second)
        send_rows(here, here, sib)
    for oth in (other, 1 - other):
        for pz in every_z:
            rows_arrived(slot(0, 1 - c, oth, pz))
    for copy in in_copies:
        copy.wait()

    contract = (((1,), (1,)), ((), ()))
    strip = 2 * tokens
    mine = lax.broadcasted_iota(jnp.int32, (strip, lanes), 1) == place

    def compute(half):
        base = half * half_rows
        grad_rows = rows_buf[base : base + half_rows, 0:width]
        x_rows = rows_buf[base : base + half_rows, width : 2 * width]
        pre_buf[...] = lax.dot_general(
            x_rows, stack_w[...], contract, preferred_element_type=f32
        )
        back_buf[...] = lax.dot_general(
            grad_rows, down_w[...], contract, preferred_element_type=f32
        )

        def elementwise(i, carry):
            at = pl.ds(pl.multiple_of(i * strip, strip), strip)
            full = pl.ds(pl.multiple_of(base + i * strip, strip), strip)
            weight = jnp.sum(
                jnp.where(mine, rows_buf[full, 2 * width :].astype(f32), 0.0),
                axis=1,
                keepdims=True,
            )
            gate_pre = pre_buf[at, 0:share]
            up_pre = pre_buf[at, share:]
            backward = back_buf[at, :]
            sigmoid_gate = jax.nn.sigmoid(gate_pre)
            activated = gate_pre * sigmoid_gate
            hidden = activated * up_pre
            comb = jnp.sum(backward * hidden, axis=1, keepdims=True)
            grad_hidden = weight * backward
            act_buf[at, 0:share] = (
                grad_hidden * up_pre * sigmoid_gate * (1.0 + gate_pre * (1.0 - sigmoid_gate))
            ).astype(bf16)
            act_buf[at, share:] = (grad_hidden * activated).astype(bf16)
            hid_buf[at, :] = (weight * hidden).astype(bf16)
            terms[full, width:] = jnp.where(mine, comb, 0.0).astype(bf16)
            return carry

        lax.fori_loop(0, half_rows // strip, elementwise, 0)
        tile = 512

        def back_tile(i, carry):
            cols = pl.ds(pl.multiple_of(i * tile, tile), tile)
            terms[base : base + half_rows, cols] = jnp.dot(
                act_buf[...], stack_w[:, cols], preferred_element_type=f32
            ).astype(bf16)
            return carry

        lax.fori_loop(0, width // tile, back_tile, 0)

    def fam_at(half, fam):
        return pl.ds(pl.multiple_of(half * half_rows + fam * fam_rows, fam_rows), fam_rows)

    def group_at(half, oth):
        return pl.ds(
            pl.multiple_of(half * half_rows + c * fam_rows + oth * group_rows, group_rows),
            group_rows,
        )

    def to_sib(half):
        send(terms.at[fam_at(half, 1 - c)], from_sib.at[half], sib_sems.at[half], sib)

    def transpose(half):
        cols = slice(half * half_rows, (half + 1) * half_rows)
        act_t[:, cols] = act_buf[...].T
        hid_t[:, cols] = hid_buf[...].T

    def add_group(half, oth, others):
        def add(i, carry):
            at = half * half_rows + c * fam_rows + oth * group_rows + i * tokens
            at = pl.ds(pl.multiple_of(at, tokens), tokens)
            sib_at = pl.ds(pl.multiple_of(oth * group_rows + i * tokens, tokens), tokens)
            rest = pl.ds(pl.multiple_of(i * tokens, tokens), tokens)
            total = terms[at, :].astype(f32) + from_sib[half, sib_at, :].astype(f32)
            for ref in others:
                total += ref[rest, :].astype(f32)
            terms[at, :] = total.astype(bf16)
            return carry

        lax.fori_loop(0, 4, add, 0)

    def to_first(half):
        arrived(from_sib.at[half], sib_sems.at[half])
        add_group(half, 1 - other, [])
        send(terms.at[group_at(half, 1 - other)], from_first.at[half], first_sems.at[half], first)

    def weight_tiles(left, right_start, out):
        tile = 512

        def step(i, carry):
            cols = pl.ds(pl.multiple_of(i * tile, tile), tile)
            right = pl.ds(pl.multiple_of(right_start + i * tile, BLOCK), tile)
            out[:, cols] = jnp.dot(
                left[...], rows_buf[:, right], preferred_element_type=f32
            ).astype(bf16)
            return carry

        lax.fori_loop(0, width // tile, step, 0)

    compute(0)
    to_sib(0)
    transpose(0)
    for oth in (other, 1 - other):
        for pz in every_z:
            here = slot(1, c, oth, pz)
            rows_arrived(here)
            send_rows(here, here, sib)
    to_first(0)
    for oth in (other, 1 - other):
        for pz in every_z:
            rows_arrived(slot(1, 1 - c, oth, pz))
    compute(1)
    to_sib(1)
    transpose(1)
    weight_tiles(hid_t, 0, down_out)
    out_copies = [pltpu.make_async_copy(down_out, grad_down_hbm.at[0], local_sems.at[3])]
    out_copies[0].start()
    to_first(1)
    weight_tiles(act_t.at[pl.ds(0, share)], width, stack_out.at[pl.ds(0, share)])
    out_copies.append(
        pltpu.make_async_copy(stack_out.at[pl.ds(0, share)], grad_gate_hbm.at[0], local_sems.at[4])
    )
    out_copies[1].start()
    for half in (1, 0):
        arrived(from_first.at[half], first_sems.at[half])
    add_group(1, other, [from_first.at[1]])
    send(terms.at[group_at(1, other)], from_second, second_sem, second)
    weight_tiles(act_t.at[pl.ds(share, share)], width, stack_out.at[pl.ds(share, share)])
    out_copies.append(
        pltpu.make_async_copy(
            stack_out.at[pl.ds(share, share)], grad_up_hbm.at[0], local_sems.at[5]
        )
    )
    out_copies[2].start()
    arrived(from_second, second_sem)
    add_group(0, other, [from_first.at[0], from_second])
    for k in range(3):
        send(
            terms.at[at_slot(slot(0, c, other, peer_z[k]))], from_z.at[k], z_sems.at[k], peers[k]
        )
    for k in range(3):
        arrived(from_z.at[k], z_sems.at[k])
    total = terms[own_rows, :].astype(f32)
    for k in range(3):
        total += from_z[k].astype(f32)
    grad_in_ref[...] = total[:, 0:width].astype(bf16)
    place_k = lax.broadcasted_iota(jnp.int32, (tokens, picks), 1)
    comb_out = jnp.zeros((tokens, picks), f32)
    for k in range(picks):
        value = jnp.sum(
            jnp.where(lane == ids[:, k : k + 1], total[:, width:], 0.0), axis=1, keepdims=True
        )
        comb_out += jnp.where(place_k == k, value, 0.0)
    comb_ref[...] = comb_out
    for copy in sent:
        copy.wait_send()
    for copy in out_copies:
        copy.wait()


def fused_body(grad_out, x_codes, x_scales, combine, expert_ids, w_gate, w_up, w_down):
    tokens, picks = expert_ids.shape
    width, share = grad_out.shape[1], w_gate.shape[1]
    experts = w_gate.shape[0] * lax.axis_size("expert")
    lanes = -(-experts // BLOCK) * BLOCK
    bf16, f32 = jnp.bfloat16, jnp.float32
    back = width + lanes
    vmem = pl.BlockSpec(memory_space=pltpu.VMEM)
    hbm = pl.BlockSpec(memory_space=pl.ANY)
    dma = pltpu.SemaphoreType.DMA
    return pl.pallas_call(
        functools.partial(expert_kernel, tokens, width, share, lanes, picks),
        out_shape=(
            jax.ShapeDtypeStruct(grad_out.shape, bf16),
            jax.ShapeDtypeStruct(combine.shape, f32),
            jax.ShapeDtypeStruct(w_gate.shape, bf16),
            jax.ShapeDtypeStruct(w_up.shape, bf16),
            jax.ShapeDtypeStruct(w_down.shape, bf16),
        ),
        in_specs=[vmem] * 5 + [hbm] * 3,
        out_specs=(vmem, vmem, hbm, hbm, hbm),
        scratch_shapes=[
            pltpu.VMEM((32 * tokens, 2 * width + lanes), bf16),
            pltpu.VMEM((2 * share, width), bf16),
            pltpu.VMEM((share, width), bf16),
            pltpu.VMEM((16 * tokens, 2 * share), f32),
            pltpu.VMEM((16 * tokens, share), f32),
            pltpu.VMEM((16 * tokens, 2 * share), bf16),
            pltpu.VMEM((16 * tokens, share), bf16),
            pltpu.VMEM((2 * share, 32 * tokens), bf16),
            pltpu.VMEM((share, 32 * tokens), bf16),
            pltpu.VMEM((2 * share, width), bf16),
            pltpu.VMEM((share, width), bf16),
            pltpu.VMEM((32 * tokens, back), bf16),
            pltpu.VMEM((2, 8 * tokens, back), bf16),
            pltpu.VMEM((2, 4 * tokens, back), bf16),
            pltpu.VMEM((4 * tokens, back), bf16),
            pltpu.VMEM((3, tokens, back), bf16),
            dma((48,)),
            dma((32,)),
            dma((2,)),
            dma((2,)),
            dma,
            dma((3,)),
            dma((6,)),
        ],
        compiler_params=pltpu.CompilerParams(
            collective_id=0, has_side_effects=True, vmem_limit_bytes=48 * 1024 * 1024
        ),
    )(grad_out, x_codes, x_scales, combine, expert_ids, w_gate, w_up, w_down)


def chosen_body(grad_out, x_codes, x_scales, combine, expert_ids, w_gate, w_up, w_down):
    tokens, picks = expert_ids.shape
    experts = w_gate.shape[0] * lax.axis_size("expert")
    capacity = min(tokens, max(2, 2 * tokens * picks // experts))
    sizes = (lax.axis_size("dp"), lax.axis_size("expert"), w_gate.shape[0])
    chosen = fused_body if capacity == tokens and sizes == (2, 16, 1) else body
    return chosen(grad_out, x_codes, x_scales, combine, expert_ids, w_gate, w_up, w_down)


def solution(mesh):
    in_specs = (
        P(("dp", "expert"), None),
        P(("dp", "expert"), None),
        P(("dp", "expert"), None),
        P(("dp", "expert"), None),
        P(("dp", "expert"), None),
        P("expert", "dp", None),
        P("expert", "dp", None),
        P("expert", "dp", None),
    )
    out_specs = (
        P(("dp", "expert"), None),
        P(("dp", "expert"), None),
        P("expert", "dp", None),
        P("expert", "dp", None),
        P("expert", "dp", None),
    )
    return jax.shard_map(chosen_body, mesh=mesh, in_specs=in_specs, out_specs=out_specs, check_vma=False)
```

```python
import functools

import jax
import jax.numpy as jnp
from jax import lax
from jax.experimental import pallas as pl
from jax.experimental.pallas import tpu as pltpu
from jax.sharding import PartitionSpec as P

BLOCK = 128
MESH = pl.DeviceIdType.MESH


def slot_table(flat_ids, experts, capacity):
    onehot = (flat_ids[:, None] == jnp.arange(experts, dtype=jnp.int32)[None, :]).astype(jnp.int32)
    before = jnp.cumsum(onehot, axis=0) - onehot
    position = jnp.sum(before * onehot, axis=1)
    slot_index = flat_ids * capacity + position
    return jnp.arange(experts * capacity, dtype=jnp.int32)[:, None] == slot_index[None, :]


def token_owner(placed, tokens, picks):
    return jnp.sum(placed.reshape(placed.shape[0], tokens, picks).astype(jnp.int32), axis=2)


def build_rows(grad_out, x_codes, x_scales, combine, expert_ids, experts, capacity):
    tokens, picks = expert_ids.shape
    placed = slot_table(expert_ids.reshape(-1), experts, capacity)
    owner = token_owner(placed, tokens, picks).astype(jnp.bfloat16)
    grad_rows = jnp.dot(owner, grad_out, preferred_element_type=jnp.float32).astype(jnp.bfloat16)
    code_rows = jnp.dot(owner, x_codes, preferred_element_type=jnp.float32).astype(jnp.bfloat16)
    scale_rows = jnp.dot(owner, x_scales, preferred_element_type=jnp.float32).astype(jnp.bfloat16)
    weight_rows = jnp.dot(
        placed.astype(jnp.bfloat16), combine.reshape(-1), preferred_element_type=jnp.float32
    ).astype(jnp.bfloat16)
    return (
        grad_rows.reshape(experts, capacity, -1),
        code_rows.reshape(experts, capacity, -1),
        scale_rows.reshape(experts, capacity, -1),
        weight_rows.reshape(experts, capacity),
    )


def body(grad_out, x_codes, x_scales, combine, expert_ids, w_gate, w_up, w_down):
    tokens, picks = expert_ids.shape
    width = grad_out.shape[1]
    groups = lax.axis_size("dp")
    experts = w_gate.shape[0] * lax.axis_size("expert")
    capacity = min(tokens, max(2, 2 * tokens * picks // experts))
    grad_rows, code_rows, scale_rows, weight_rows = build_rows(
        grad_out, x_codes, x_scales, combine, expert_ids, experts, capacity
    )
    grad_rows, code_rows, scale_rows, weight_rows = (
        lax.all_to_all(grad_rows, "expert", split_axis=0, concat_axis=0, tiled=True),
        lax.all_to_all(code_rows, "expert", split_axis=0, concat_axis=0, tiled=True),
        lax.all_to_all(scale_rows, "expert", split_axis=0, concat_axis=0, tiled=True),
        lax.all_to_all(weight_rows, "expert", split_axis=0, concat_axis=0, tiled=True),
    )
    grad_rows, code_rows, scale_rows, weight_rows = (
        lax.all_gather(grad_rows[None], "dp", axis=0, tiled=True),
        lax.all_gather(code_rows[None], "dp", axis=0, tiled=True),
        lax.all_gather(scale_rows[None], "dp", axis=0, tiled=True),
        lax.all_gather(weight_rows[None], "dp", axis=0, tiled=True),
    )
    rows = groups * experts * capacity
    scale_count = width // BLOCK
    grad_flat = grad_rows.reshape(rows, width)
    x_rows = (
        (
            code_rows.reshape(rows, scale_count, BLOCK).astype(jnp.float32)
            * scale_rows.reshape(rows, scale_count, 1).astype(jnp.float32)
        )
        .reshape(rows, width)
        .astype(jnp.bfloat16)
    )
    weight_flat = weight_rows.reshape(rows).astype(jnp.float32)
    share = w_gate.shape[1]
    stacked_w = jnp.concatenate([w_gate[0], w_up[0]], axis=0)
    down_w = w_down[0]
    both_pre = lax.dot_general(
        x_rows, stacked_w, (((1,), (1,)), ((), ())), preferred_element_type=jnp.float32
    )
    gate_pre = both_pre[:, :share]
    up_pre = both_pre[:, share:]
    sigmoid_gate = jax.nn.sigmoid(gate_pre)
    activated = gate_pre * sigmoid_gate
    hidden = (activated * up_pre).astype(jnp.bfloat16)
    scaled = (weight_flat[:, None] * grad_flat.astype(jnp.float32)).astype(jnp.bfloat16)
    backward = lax.dot_general(
        grad_flat, down_w, (((1,), (1,)), ((), ())), preferred_element_type=jnp.float32
    )
    partial_comb = jnp.sum(backward * hidden.astype(jnp.float32), axis=1)
    grad_hidden = weight_flat[:, None] * backward
    grad_gate_pre = (
        grad_hidden * up_pre * sigmoid_gate * (1.0 + gate_pre * (1.0 - sigmoid_gate))
    ).astype(jnp.bfloat16)
    grad_up_pre = (grad_hidden * activated).astype(jnp.bfloat16)
    grad_both_pre = jnp.concatenate([grad_gate_pre, grad_up_pre], axis=1)
    grad_down = lax.dot_general(
        hidden, scaled, (((0,), (0,)), ((), ())), preferred_element_type=jnp.float32
    ).astype(jnp.bfloat16)
    grad_stacked = lax.dot_general(
        grad_both_pre, x_rows, (((0,), (0,)), ((), ())), preferred_element_type=jnp.float32
    ).astype(jnp.bfloat16)
    grad_gate = grad_stacked[:share]
    grad_up = grad_stacked[share:]
    input_part = jnp.dot(grad_both_pre, stacked_w, preferred_element_type=jnp.float32)
    summed = lax.psum_scatter(
        input_part.reshape(groups, experts, capacity, width).astype(jnp.bfloat16),
        "dp",
        scatter_dimension=0,
        tiled=True,
    ).astype(jnp.float32)
    comb_all = lax.psum(partial_comb, "dp")
    own_terms = lax.dynamic_slice_in_dim(
        comb_all, lax.axis_index("dp") * (experts * capacity), experts * capacity
    )
    back_grad, back_comb = (
        lax.all_to_all(
            summed.reshape(experts, capacity, width).astype(jnp.bfloat16),
            "expert",
            split_axis=0,
            concat_axis=0,
            tiled=True,
        ).astype(jnp.float32),
        lax.all_to_all(
            own_terms.reshape(experts, capacity).astype(jnp.bfloat16),
            "expert",
            split_axis=0,
            concat_axis=0,
            tiled=True,
        ).astype(jnp.float32),
    )
    placed = slot_table(expert_ids.reshape(-1), experts, capacity)
    owner = token_owner(placed, tokens, picks).astype(jnp.float32)
    grad_in = lax.dot_general(
        owner,
        back_grad.reshape(experts * capacity, width),
        (((0,), (0,)), ((), ())),
        precision=lax.Precision.HIGHEST,
    ).astype(jnp.bfloat16)
    grad_combine = lax.dot_general(
        placed.astype(jnp.float32),
        back_comb.reshape(experts * capacity),
        (((0,), (0,)), ((), ())),
        precision=lax.Precision.HIGHEST,
    ).reshape(tokens, picks)
    return (grad_in, grad_combine, grad_gate[None], grad_up[None], grad_down[None])


def expert_kernel(
    tokens,
    width,
    share,
    lanes,
    picks,
    grad_hbm,
    codes_hbm,
    scales_hbm,
    ids_hbm,
    combine_ref,
    gate_hbm,
    up_hbm,
    down_hbm,
    grad_in_ref,
    comb_ref,
    grad_gate_ref,
    grad_up_ref,
    grad_down_ref,
    codes_ref,
    scales_ref,
    ids_ref,
    rows_buf,
    stack_w,
    down_w,
    pre_buf,
    back_buf,
    act_buf,
    hid_buf,
    act_t,
    hid_t,
    terms,
    from_sib,
    from_first,
    from_second,
    from_z,
    send_sems,
    row_sems,
    sib_sems,
    first_sems,
    second_sem,
    z_sems,
    local_sems,
):
    f32, bf16 = jnp.float32, jnp.bfloat16
    half_rows, fam_rows, group_rows = 16 * tokens, 8 * tokens, 4 * tokens
    x = lax.axis_index("dp")
    place = lax.axis_index("expert")
    z, y, c = place // 4, (place // 2) % 2, place % 2

    def device(dx, dz, dy, dc):
        return (dx, dz * 4 + dy * 2 + dc)

    sib = device(x, z, y, 1 - c)
    first = device(x + (1 - c) * (1 - 2 * x), z, y + c * (1 - 2 * y), c)
    second = device(x + c * (1 - 2 * x), z, y + (1 - c) * (1 - 2 * y), c)
    peer_z = [z + 1 - 2 * (z % 2), z + 2 - 4 * (z // 2), 3 - z]
    peers = [device(x, pz, y, c) for pz in peer_z]
    other = x + c * (y - x)

    in_copies = [
        pltpu.make_async_copy(gate_hbm.at[0], stack_w.at[pl.ds(0, share)], local_sems.at[0]),
        pltpu.make_async_copy(up_hbm.at[0], stack_w.at[pl.ds(share, share)], local_sems.at[1]),
        pltpu.make_async_copy(down_hbm.at[0], down_w, local_sems.at[2]),
    ]
    own = z + 4 * (2 * c + other)
    own_rows = pl.ds(pl.multiple_of(own * tokens, tokens), tokens)
    own_copies = [
        pltpu.make_async_copy(codes_hbm, codes_ref, local_sems.at[3]),
        pltpu.make_async_copy(scales_hbm, scales_ref, local_sems.at[4]),
        pltpu.make_async_copy(ids_hbm, ids_ref, local_sems.at[5]),
        pltpu.make_async_copy(grad_hbm, rows_buf.at[own_rows, pl.ds(0, width)], local_sems.at[6]),
    ]
    for copy in own_copies + in_copies:
        copy.start()

    barrier = pltpu.get_barrier_semaphore()
    for partner in [sib, first, second] + peers:
        pl.semaphore_signal(barrier, inc=1, device_id=partner, device_id_type=MESH)

    def slot(half, fam, oth, zz):
        return half * 16 + fam * 8 + oth * 4 + zz

    def at_slot(index):
        return pl.ds(pl.multiple_of(index * tokens, tokens), tokens)

    for copy in own_copies:
        copy.wait()
    scales = scales_ref[...].astype(f32)
    for b in range(width // BLOCK):
        cols = slice(b * BLOCK, (b + 1) * BLOCK)
        rows_buf[own_rows, width + b * BLOCK : width + (b + 1) * BLOCK] = (
            codes_ref[:, cols].astype(f32) * scales[:, b : b + 1]
        ).astype(bf16)
    lane = lax.broadcasted_iota(jnp.int32, (tokens, lanes), 1)
    eye = lax.broadcasted_iota(jnp.int32, (tokens, tokens), 0) == lax.broadcasted_iota(
        jnp.int32, (tokens, tokens), 1
    )

    def column(row):
        return jnp.sum(jnp.where(eye, row, jnp.zeros_like(row)), axis=1, keepdims=True)

    combine = combine_ref[...].astype(f32)
    ids = [column(ids_ref[k : k + 1, :]) for k in range(picks)]
    weight_row = jnp.zeros((tokens, lanes), f32)
    for k in range(picks):
        weight_row += jnp.where(lane == ids[k], column(combine[k : k + 1, :]), 0.0)
    rows_buf[own_rows, 2 * width :] = weight_row.astype(bf16)

    pl.semaphore_wait(barrier, 6)

    sent = []

    def send(src, dst, sem, to, only=None):
        copy = pltpu.make_async_remote_copy(
            src_ref=src,
            dst_ref=dst,
            send_sem=send_sems.at[len(sent)],
            recv_sem=sem,
            device_id=to,
            device_id_type=MESH,
        )
        sent.append((copy, only))
        if only is None:
            copy.start()
        else:
            pl.when(only)(copy.start)

    def arrived(ref, sem):
        pltpu.make_async_remote_copy(
            src_ref=ref,
            dst_ref=ref,
            send_sem=send_sems.at[0],
            recv_sem=sem,
            device_id=sib,
            device_id_type=MESH,
        ).wait_recv()

    def send_rows(src, dst, to, only=None):
        send(rows_buf.at[at_slot(src)], rows_buf.at[at_slot(dst)], row_sems.at[dst], to, only)

    def rows_arrived(index):
        arrived(rows_buf.at[at_slot(index)], row_sems.at[index])

    middle = (z == 1) | (z == 2)
    near, across = peers[0], peers[2]
    by_arrival = [peer_z[0], 2 - z // 2, 3 - 3 * (z // 2)]
    every_z = [z] + by_arrival
    send_rows(own, own, near)
    send_rows(own, own, across, middle)
    send_rows(own, own, first)
    send_rows(own, own + 16, second)
    send_rows(own, own, sib)
    for pz, onward in zip(by_arrival, (across, near, near)):
        here = slot(0, c, other, pz)
        rows_arrived(here)
        send_rows(here, here, onward, middle)
        send_rows(here, here, first)
        send_rows(here, here + 16, second)
        send_rows(here, here, sib)
    for pz in every_z:
        here = slot(0, c, 1 - other, pz)
        rows_arrived(here)
        send_rows(here, here + 16, second)
        send_rows(here, here, sib)
    for oth in (other, 1 - other):
        for pz in every_z:
            rows_arrived(slot(0, 1 - c, oth, pz))
    for copy in in_copies:
        copy.wait()

    contract = (((1,), (1,)), ((), ()))
    strip = 2 * tokens
    mine = lax.broadcasted_iota(jnp.int32, (strip, lanes), 1) == place

    def compute(half):
        base = half * half_rows
        grad_rows = rows_buf[base : base + half_rows, 0:width]
        x_rows = rows_buf[base : base + half_rows, width : 2 * width]
        pre_buf[...] = lax.dot_general(
            x_rows, stack_w[...], contract, preferred_element_type=f32
        )
        back_buf[...] = lax.dot_general(
            grad_rows, down_w[...], contract, preferred_element_type=f32
        )

        def elementwise(i, carry):
            at = pl.ds(pl.multiple_of(i * strip, strip), strip)
            full = pl.ds(pl.multiple_of(base + i * strip, strip), strip)
            weight = jnp.sum(
                jnp.where(mine, rows_buf[full, 2 * width :].astype(f32), 0.0),
                axis=1,
                keepdims=True,
            )
            gate_pre = pre_buf[at, 0:share]
            up_pre = pre_buf[at, share:]
            backward = back_buf[at, :]
            sigmoid_gate = jax.nn.sigmoid(gate_pre)
            activated = gate_pre * sigmoid_gate
            hidden = activated * up_pre
            comb = jnp.sum(backward * hidden, axis=1, keepdims=True)
            grad_hidden = weight * backward
            act_buf[at, 0:share] = (
                grad_hidden * up_pre * sigmoid_gate * (1.0 + gate_pre * (1.0 - sigmoid_gate))
            ).astype(bf16)
            act_buf[at, share:] = (grad_hidden * activated).astype(bf16)
            hid_buf[at, :] = (weight * hidden).astype(bf16)
            terms[full, width:] = jnp.where(mine, comb, 0.0).astype(bf16)
            return carry

        lax.fori_loop(0, half_rows // strip, elementwise, 0)
        tile = 512

        def back_tile(i, carry):
            cols = pl.ds(pl.multiple_of(i * tile, tile), tile)
            terms[base : base + half_rows, cols] = jnp.dot(
                act_buf[...], stack_w[:, cols], preferred_element_type=f32
            ).astype(bf16)
            return carry

        lax.fori_loop(0, width // tile, back_tile, 0)

    def fam_at(half, fam):
        return pl.ds(pl.multiple_of(half * half_rows + fam * fam_rows, fam_rows), fam_rows)

    def group_at(half, oth):
        return pl.ds(
            pl.multiple_of(half * half_rows + c * fam_rows + oth * group_rows, group_rows),
            group_rows,
        )

    def to_sib(half):
        send(terms.at[fam_at(half, 1 - c)], from_sib.at[half], sib_sems.at[half], sib)

    def transpose(half):
        cols = slice(half * half_rows, (half + 1) * half_rows)
        act_t[:, cols] = act_buf[...].T
        hid_t[:, cols] = hid_buf[...].T

    def add_group(half, oth, others):
        def add(i, carry):
            at = half * half_rows + c * fam_rows + oth * group_rows + i * tokens
            at = pl.ds(pl.multiple_of(at, tokens), tokens)
            sib_at = pl.ds(pl.multiple_of(oth * group_rows + i * tokens, tokens), tokens)
            rest = pl.ds(pl.multiple_of(i * tokens, tokens), tokens)
            total = terms[at, :].astype(f32) + from_sib[half, sib_at, :].astype(f32)
            for ref in others:
                total += ref[rest, :].astype(f32)
            terms[at, :] = total.astype(bf16)
            return carry

        lax.fori_loop(0, 4, add, 0)

    def to_first(half):
        arrived(from_sib.at[half], sib_sems.at[half])
        add_group(half, 1 - other, [])
        send(terms.at[group_at(half, 1 - other)], from_first.at[half], first_sems.at[half], first)

    def weight_tiles(left, right_start, out):
        tile = 512

        def step(i, carry):
            cols = pl.ds(pl.multiple_of(i * tile, tile), tile)
            right = pl.ds(pl.multiple_of(right_start + i * tile, BLOCK), tile)
            out[0, :, cols] = jnp.dot(
                left[...], rows_buf[:, right], preferred_element_type=f32
            ).astype(bf16)
            return carry

        lax.fori_loop(0, width // tile, step, 0)

    compute(0)
    to_sib(0)
    transpose(0)
    for oth in (other, 1 - other):
        for pz in every_z:
            here = slot(1, c, oth, pz)
            rows_arrived(here)
            send_rows(here, here, sib)
    to_first(0)
    for oth in (other, 1 - other):
        for pz in every_z:
            rows_arrived(slot(1, 1 - c, oth, pz))
    compute(1)
    to_sib(1)
    transpose(1)
    weight_tiles(hid_t, 0, grad_down_ref)
    to_first(1)
    weight_tiles(act_t.at[pl.ds(0, share)], width, grad_gate_ref)
    for half in (1, 0):
        arrived(from_first.at[half], first_sems.at[half])
    add_group(1, other, [from_first.at[1]])
    send(terms.at[group_at(1, other)], from_second, second_sem, second)
    weight_tiles(act_t.at[pl.ds(share, share)], width, grad_up_ref)
    arrived(from_second, second_sem)
    add_group(0, other, [from_first.at[0], from_second])
    for k in range(3):
        send(
            terms.at[at_slot(slot(0, c, other, peer_z[k]))], from_z.at[k], z_sems.at[k], peers[k]
        )
    for k in range(3):
        arrived(from_z.at[k], z_sems.at[k])
    total = terms[own_rows, :].astype(f32)
    for k in range(3):
        total += from_z[k].astype(f32)
    grad_in_ref[...] = total[:, 0:width].astype(bf16)
    place_k = lax.broadcasted_iota(jnp.int32, (picks, tokens), 0)
    comb_out = jnp.zeros((picks, tokens), f32)
    for k in range(picks):
        value = jnp.sum(
            jnp.where(lane == ids[k], total[:, width:], 0.0), axis=1, keepdims=True
        )
        value = jnp.sum(jnp.where(eye, value, 0.0), axis=0, keepdims=True)
        comb_out += jnp.where(place_k == k, value, 0.0)
    comb_ref[...] = comb_out
    for copy, only in sent:
        if only is None:
            copy.wait_send()
        else:
            pl.when(only)(copy.wait_send)


def fused_body(grad_out, x_codes, x_scales, combine, expert_ids, w_gate, w_up, w_down):
    tokens, picks = expert_ids.shape
    width, share = grad_out.shape[1], w_gate.shape[1]
    experts = w_gate.shape[0] * lax.axis_size("expert")
    lanes = -(-experts // BLOCK) * BLOCK
    bf16, f32 = jnp.bfloat16, jnp.float32
    back = width + lanes
    vmem = pl.BlockSpec(memory_space=pltpu.VMEM)
    hbm = pl.BlockSpec(memory_space=pltpu.HBM)
    dma = pltpu.SemaphoreType.DMA
    outs = pl.pallas_call(
        functools.partial(expert_kernel, tokens, width, share, lanes, picks),
        out_shape=(
            jax.ShapeDtypeStruct(grad_out.shape, bf16),
            jax.ShapeDtypeStruct((picks, tokens), f32),
            jax.ShapeDtypeStruct(w_gate.shape, bf16),
            jax.ShapeDtypeStruct(w_up.shape, bf16),
            jax.ShapeDtypeStruct(w_down.shape, bf16),
        ),
        in_specs=[hbm] * 4 + [vmem] + [hbm] * 3,
        out_specs=(vmem,) * 5,
        scratch_shapes=[
            pltpu.VMEM(x_codes.shape, bf16),
            pltpu.VMEM(x_scales.shape, bf16),
            pltpu.VMEM((picks, tokens), jnp.int32),
            pltpu.VMEM((32 * tokens, 2 * width + lanes), bf16),
            pltpu.VMEM((2 * share, width), bf16),
            pltpu.VMEM((share, width), bf16),
            pltpu.VMEM((16 * tokens, 2 * share), f32),
            pltpu.VMEM((16 * tokens, share), f32),
            pltpu.VMEM((16 * tokens, 2 * share), bf16),
            pltpu.VMEM((16 * tokens, share), bf16),
            pltpu.VMEM((2 * share, 32 * tokens), bf16),
            pltpu.VMEM((share, 32 * tokens), bf16),
            pltpu.VMEM((32 * tokens, back), bf16),
            pltpu.VMEM((2, 8 * tokens, back), bf16),
            pltpu.VMEM((2, 4 * tokens, back), bf16),
            pltpu.VMEM((4 * tokens, back), bf16),
            pltpu.VMEM((3, tokens, back), bf16),
            dma((64,)),
            dma((32,)),
            dma((2,)),
            dma((2,)),
            dma,
            dma((3,)),
            dma((7,)),
        ],
        compiler_params=pltpu.CompilerParams(
            collective_id=0, has_side_effects=True, vmem_limit_bytes=48 * 1024 * 1024
        ),
    )(grad_out, x_codes, x_scales, expert_ids.T, combine.T, w_gate, w_up, w_down)
    return (outs[0], outs[1].T) + tuple(outs[2:])


def chosen_body(grad_out, x_codes, x_scales, combine, expert_ids, w_gate, w_up, w_down):
    tokens, picks = expert_ids.shape
    experts = w_gate.shape[0] * lax.axis_size("expert")
    capacity = min(tokens, max(2, 2 * tokens * picks // experts))
    sizes = (lax.axis_size("dp"), lax.axis_size("expert"), w_gate.shape[0])
    chosen = fused_body if capacity == tokens and sizes == (2, 16, 1) else body
    return chosen(grad_out, x_codes, x_scales, combine, expert_ids, w_gate, w_up, w_down)


def solution(mesh):
    in_specs = (
        P(("dp", "expert"), None),
        P(("dp", "expert"), None),
        P(("dp", "expert"), None),
        P(("dp", "expert"), None),
        P(("dp", "expert"), None),
        P("expert", "dp", None),
        P("expert", "dp", None),
        P("expert", "dp", None),
    )
    out_specs = (
        P(("dp", "expert"), None),
        P(("dp", "expert"), None),
        P("expert", "dp", None),
        P("expert", "dp", None),
        P("expert", "dp", None),
    )
    return jax.shard_map(chosen_body, mesh=mesh, in_specs=in_specs, out_specs=out_specs, check_vma=False)
```

```python
import functools

import jax
import jax.numpy as jnp
from jax import lax
from jax.experimental import pallas as pl
from jax.experimental.pallas import tpu as pltpu
from jax.sharding import PartitionSpec as P

BLOCK = 128
MESH = pl.DeviceIdType.MESH


def slot_table(flat_ids, experts, capacity):
    onehot = (flat_ids[:, None] == jnp.arange(experts, dtype=jnp.int32)[None, :]).astype(jnp.int32)
    before = jnp.cumsum(onehot, axis=0) - onehot
    position = jnp.sum(before * onehot, axis=1)
    slot_index = flat_ids * capacity + position
    return jnp.arange(experts * capacity, dtype=jnp.int32)[:, None] == slot_index[None, :]


def token_owner(placed, tokens, picks):
    return jnp.sum(placed.reshape(placed.shape[0], tokens, picks).astype(jnp.int32), axis=2)


def build_rows(grad_out, x_codes, x_scales, combine, expert_ids, experts, capacity):
    tokens, picks = expert_ids.shape
    placed = slot_table(expert_ids.reshape(-1), experts, capacity)
    owner = token_owner(placed, tokens, picks).astype(jnp.bfloat16)
    grad_rows = jnp.dot(owner, grad_out, preferred_element_type=jnp.float32).astype(jnp.bfloat16)
    code_rows = jnp.dot(owner, x_codes, preferred_element_type=jnp.float32).astype(jnp.bfloat16)
    scale_rows = jnp.dot(owner, x_scales, preferred_element_type=jnp.float32).astype(jnp.bfloat16)
    weight_rows = jnp.dot(
        placed.astype(jnp.bfloat16), combine.reshape(-1), preferred_element_type=jnp.float32
    ).astype(jnp.bfloat16)
    return (
        grad_rows.reshape(experts, capacity, -1),
        code_rows.reshape(experts, capacity, -1),
        scale_rows.reshape(experts, capacity, -1),
        weight_rows.reshape(experts, capacity),
    )


def body(grad_out, x_codes, x_scales, combine, expert_ids, w_gate, w_up, w_down):
    tokens, picks = expert_ids.shape
    width = grad_out.shape[1]
    groups = lax.axis_size("dp")
    experts = w_gate.shape[0] * lax.axis_size("expert")
    capacity = min(tokens, max(2, 2 * tokens * picks // experts))
    grad_rows, code_rows, scale_rows, weight_rows = build_rows(
        grad_out, x_codes, x_scales, combine, expert_ids, experts, capacity
    )
    grad_rows, code_rows, scale_rows, weight_rows = (
        lax.all_to_all(grad_rows, "expert", split_axis=0, concat_axis=0, tiled=True),
        lax.all_to_all(code_rows, "expert", split_axis=0, concat_axis=0, tiled=True),
        lax.all_to_all(scale_rows, "expert", split_axis=0, concat_axis=0, tiled=True),
        lax.all_to_all(weight_rows, "expert", split_axis=0, concat_axis=0, tiled=True),
    )
    grad_rows, code_rows, scale_rows, weight_rows = (
        lax.all_gather(grad_rows[None], "dp", axis=0, tiled=True),
        lax.all_gather(code_rows[None], "dp", axis=0, tiled=True),
        lax.all_gather(scale_rows[None], "dp", axis=0, tiled=True),
        lax.all_gather(weight_rows[None], "dp", axis=0, tiled=True),
    )
    rows = groups * experts * capacity
    scale_count = width // BLOCK
    grad_flat = grad_rows.reshape(rows, width)
    x_rows = (
        (
            code_rows.reshape(rows, scale_count, BLOCK).astype(jnp.float32)
            * scale_rows.reshape(rows, scale_count, 1).astype(jnp.float32)
        )
        .reshape(rows, width)
        .astype(jnp.bfloat16)
    )
    weight_flat = weight_rows.reshape(rows).astype(jnp.float32)
    share = w_gate.shape[1]
    stacked_w = jnp.concatenate([w_gate[0], w_up[0]], axis=0)
    down_w = w_down[0]
    both_pre = lax.dot_general(
        x_rows, stacked_w, (((1,), (1,)), ((), ())), preferred_element_type=jnp.float32
    )
    gate_pre = both_pre[:, :share]
    up_pre = both_pre[:, share:]
    sigmoid_gate = jax.nn.sigmoid(gate_pre)
    activated = gate_pre * sigmoid_gate
    hidden = (activated * up_pre).astype(jnp.bfloat16)
    scaled = (weight_flat[:, None] * grad_flat.astype(jnp.float32)).astype(jnp.bfloat16)
    backward = lax.dot_general(
        grad_flat, down_w, (((1,), (1,)), ((), ())), preferred_element_type=jnp.float32
    )
    partial_comb = jnp.sum(backward * hidden.astype(jnp.float32), axis=1)
    grad_hidden = weight_flat[:, None] * backward
    grad_gate_pre = (
        grad_hidden * up_pre * sigmoid_gate * (1.0 + gate_pre * (1.0 - sigmoid_gate))
    ).astype(jnp.bfloat16)
    grad_up_pre = (grad_hidden * activated).astype(jnp.bfloat16)
    grad_both_pre = jnp.concatenate([grad_gate_pre, grad_up_pre], axis=1)
    grad_down = lax.dot_general(
        hidden, scaled, (((0,), (0,)), ((), ())), preferred_element_type=jnp.float32
    ).astype(jnp.bfloat16)
    grad_stacked = lax.dot_general(
        grad_both_pre, x_rows, (((0,), (0,)), ((), ())), preferred_element_type=jnp.float32
    ).astype(jnp.bfloat16)
    grad_gate = grad_stacked[:share]
    grad_up = grad_stacked[share:]
    input_part = jnp.dot(grad_both_pre, stacked_w, preferred_element_type=jnp.float32)
    summed = lax.psum_scatter(
        input_part.reshape(groups, experts, capacity, width).astype(jnp.bfloat16),
        "dp",
        scatter_dimension=0,
        tiled=True,
    ).astype(jnp.float32)
    comb_all = lax.psum(partial_comb, "dp")
    own_terms = lax.dynamic_slice_in_dim(
        comb_all, lax.axis_index("dp") * (experts * capacity), experts * capacity
    )
    back_grad, back_comb = (
        lax.all_to_all(
            summed.reshape(experts, capacity, width).astype(jnp.bfloat16),
            "expert",
            split_axis=0,
            concat_axis=0,
            tiled=True,
        ).astype(jnp.float32),
        lax.all_to_all(
            own_terms.reshape(experts, capacity).astype(jnp.bfloat16),
            "expert",
            split_axis=0,
            concat_axis=0,
            tiled=True,
        ).astype(jnp.float32),
    )
    placed = slot_table(expert_ids.reshape(-1), experts, capacity)
    owner = token_owner(placed, tokens, picks).astype(jnp.float32)
    grad_in = lax.dot_general(
        owner,
        back_grad.reshape(experts * capacity, width),
        (((0,), (0,)), ((), ())),
        precision=lax.Precision.HIGHEST,
    ).astype(jnp.bfloat16)
    grad_combine = lax.dot_general(
        placed.astype(jnp.float32),
        back_comb.reshape(experts * capacity),
        (((0,), (0,)), ((), ())),
        precision=lax.Precision.HIGHEST,
    ).reshape(tokens, picks)
    return (grad_in, grad_combine, grad_gate[None], grad_up[None], grad_down[None])


def expert_kernel(
    tokens,
    width,
    share,
    lanes,
    picks,
    grad_hbm,
    codes_hbm,
    scales_hbm,
    ids_hbm,
    combine_hbm,
    gate_hbm,
    up_hbm,
    down_hbm,
    grad_in_ref,
    comb_ref,
    grad_gate_hbm,
    grad_up_hbm,
    grad_down_hbm,
    codes_ref,
    scales_ref,
    ids_ref,
    combine_ref,
    rows_buf,
    stack_w,
    down_w,
    pre_buf,
    back_buf,
    act_buf,
    hid_buf,
    act_t,
    hid_t,
    stack_out,
    down_out,
    terms,
    from_sib,
    from_first,
    from_second,
    from_z,
    send_sems,
    row_sems,
    sib_sems,
    first_sems,
    second_sems,
    z_sems,
    local_sems,
):
    f32, bf16 = jnp.float32, jnp.bfloat16
    half_rows, fam_rows, group_rows = 16 * tokens, 8 * tokens, 4 * tokens
    x = lax.axis_index("dp")
    place = lax.axis_index("expert")
    z, y, c = place // 4, (place // 2) % 2, place % 2

    def device(dx, dz, dy, dc):
        return (dx, dz * 4 + dy * 2 + dc)

    sib = device(x, z, y, 1 - c)
    first = device(x + (1 - c) * (1 - 2 * x), z, y + c * (1 - 2 * y), c)
    second = device(x + c * (1 - 2 * x), z, y + (1 - c) * (1 - 2 * y), c)
    peer_z = [z + 1 - 2 * (z % 2), z + 2 - 4 * (z // 2), 3 - z]
    peers = [device(x, pz, y, c) for pz in peer_z]
    other = x + c * (y - x)

    in_copies = [
        pltpu.make_async_copy(gate_hbm.at[0], stack_w.at[pl.ds(0, share)], local_sems.at[0]),
        pltpu.make_async_copy(up_hbm.at[0], stack_w.at[pl.ds(share, share)], local_sems.at[1]),
        pltpu.make_async_copy(down_hbm.at[0], down_w, local_sems.at[2]),
    ]
    own = z + 4 * (2 * c + other)
    own_rows = pl.ds(pl.multiple_of(own * tokens, tokens), tokens)
    own_copies = [
        pltpu.make_async_copy(codes_hbm, codes_ref, local_sems.at[3]),
        pltpu.make_async_copy(scales_hbm, scales_ref, local_sems.at[4]),
        pltpu.make_async_copy(ids_hbm, ids_ref, local_sems.at[5]),
        pltpu.make_async_copy(combine_hbm, combine_ref, local_sems.at[7]),
        pltpu.make_async_copy(grad_hbm, rows_buf.at[own_rows, pl.ds(0, width)], local_sems.at[6]),
    ]
    for copy in own_copies + in_copies:
        copy.start()

    barrier = pltpu.get_barrier_semaphore()
    for partner in [sib, first, second] + peers:
        pl.semaphore_signal(barrier, inc=1, device_id=partner, device_id_type=MESH)

    def slot(half, fam, oth, zz):
        return half * 16 + fam * 8 + oth * 4 + zz

    def at_slot(index):
        return pl.ds(pl.multiple_of(index * tokens, tokens), tokens)

    for copy in own_copies:
        copy.wait()
    scales = scales_ref[...].astype(f32)
    for b in range(width // BLOCK):
        cols = slice(b * BLOCK, (b + 1) * BLOCK)
        rows_buf[own_rows, width + b * BLOCK : width + (b + 1) * BLOCK] = (
            codes_ref[:, cols].astype(f32) * scales[:, b : b + 1]
        ).astype(bf16)
    lane = lax.broadcasted_iota(jnp.int32, (tokens, lanes), 1)
    eye = lax.broadcasted_iota(jnp.int32, (tokens, tokens), 0) == lax.broadcasted_iota(
        jnp.int32, (tokens, tokens), 1
    )

    def column(row):
        return jnp.sum(jnp.where(eye, row, jnp.zeros_like(row)), axis=1, keepdims=True)

    combine = combine_ref[...].astype(f32)
    ids = [column(ids_ref[k : k + 1, :]) for k in range(picks)]
    weight_row = jnp.zeros((tokens, lanes), f32)
    for k in range(picks):
        weight_row += jnp.where(lane == ids[k], column(combine[k : k + 1, :]), 0.0)
    rows_buf[own_rows, 2 * width :] = weight_row.astype(bf16)

    pl.semaphore_wait(barrier, 6)

    sent = []

    def send(src, dst, sem, to, only=None):
        copy = pltpu.make_async_remote_copy(
            src_ref=src,
            dst_ref=dst,
            send_sem=send_sems.at[len(sent)],
            recv_sem=sem,
            device_id=to,
            device_id_type=MESH,
        )
        sent.append((copy, only))
        if only is None:
            copy.start()
        else:
            pl.when(only)(copy.start)

    def arrived(ref, sem):
        pltpu.make_async_remote_copy(
            src_ref=ref,
            dst_ref=ref,
            send_sem=send_sems.at[0],
            recv_sem=sem,
            device_id=sib,
            device_id_type=MESH,
        ).wait_recv()

    def send_rows(src, dst, to, only=None):
        send(rows_buf.at[at_slot(src)], rows_buf.at[at_slot(dst)], row_sems.at[dst], to, only)

    def rows_arrived(index):
        arrived(rows_buf.at[at_slot(index)], row_sems.at[index])

    middle = (z == 1) | (z == 2)
    near, across = peers[0], peers[2]
    by_arrival = [peer_z[0], 2 - z // 2, 3 - 3 * (z // 2)]
    every_z = [z] + by_arrival
    send_rows(own, own, near)
    send_rows(own, own, across, middle)
    send_rows(own, own, first)
    send_rows(own, own + 16, second)
    send_rows(own, own, sib)
    for pz, onward in zip(by_arrival, (across, near, near)):
        here = slot(0, c, other, pz)
        rows_arrived(here)
        send_rows(here, here, onward, middle)
        send_rows(here, here, first)
        send_rows(here, here + 16, second)
        send_rows(here, here, sib)
    for pz in every_z:
        here = slot(0, c, 1 - other, pz)
        rows_arrived(here)
        send_rows(here, here + 16, second)
        send_rows(here, here, sib)
    for oth in (other, 1 - other):
        for pz in every_z:
            rows_arrived(slot(0, 1 - c, oth, pz))
    for copy in in_copies:
        copy.wait()

    contract = (((1,), (1,)), ((), ()))
    strip = 2 * tokens
    mine = lax.broadcasted_iota(jnp.int32, (strip, lanes), 1) == place

    parts = ((0, width // 2), (width // 2, width // 2 + lanes))

    def part(h):
        return pl.ds(*parts[h])

    def compute(half):
        base = half * half_rows
        grad_rows = rows_buf[base : base + half_rows, 0:width]
        x_rows = rows_buf[base : base + half_rows, width : 2 * width]
        pre_buf[...] = lax.dot_general(
            x_rows, stack_w[...], contract, preferred_element_type=f32
        )
        back_buf[...] = lax.dot_general(
            grad_rows, down_w[...], contract, preferred_element_type=f32
        )

        def elementwise(i, carry):
            at = pl.ds(pl.multiple_of(i * strip, strip), strip)
            full = pl.ds(pl.multiple_of(base + i * strip, strip), strip)
            weight = jnp.sum(
                jnp.where(mine, rows_buf[full, 2 * width :].astype(f32), 0.0),
                axis=1,
                keepdims=True,
            )
            gate_pre = pre_buf[at, 0:share]
            up_pre = pre_buf[at, share:]
            backward = back_buf[at, :]
            sigmoid_gate = jax.nn.sigmoid(gate_pre)
            activated = gate_pre * sigmoid_gate
            hidden = activated * up_pre
            comb = jnp.sum(backward * hidden, axis=1, keepdims=True)
            grad_hidden = weight * backward
            act_buf[at, 0:share] = (
                grad_hidden * up_pre * sigmoid_gate * (1.0 + gate_pre * (1.0 - sigmoid_gate))
            ).astype(bf16)
            act_buf[at, share:] = (grad_hidden * activated).astype(bf16)
            hid_buf[at, :] = (weight * hidden).astype(bf16)
            terms[full, width:] = jnp.where(mine, comb, 0.0).astype(bf16)
            return carry

        lax.fori_loop(0, half_rows // strip, elementwise, 0)
        tile = 512

        def back_tile(i, carry):
            cols = pl.ds(pl.multiple_of(i * tile, tile), tile)
            terms[base : base + half_rows, cols] = jnp.dot(
                act_buf[...], stack_w[:, cols], preferred_element_type=f32
            ).astype(bf16)
            return carry

        tiles = width // tile
        lax.fori_loop(0, tiles // 2, back_tile, 0)
        to_sib(half, 0)
        lax.fori_loop(tiles // 2, tiles, back_tile, 0)
        to_sib(half, 1)

    def fam_at(half, fam):
        return pl.ds(pl.multiple_of(half * half_rows + fam * fam_rows, fam_rows), fam_rows)

    def group_at(half, oth):
        return pl.ds(
            pl.multiple_of(half * half_rows + c * fam_rows + oth * group_rows, group_rows),
            group_rows,
        )

    def to_sib(half, h):
        send(
            terms.at[fam_at(half, 1 - c), part(h)],
            from_sib.at[half, :, part(h)],
            sib_sems.at[2 * half + h],
            sib,
        )

    def transpose(half, source, target):
        target[:, half * half_rows : (half + 1) * half_rows] = source[...].T

    def add_group(half, oth, h, others):
        cols = part(h)

        def add(i, carry):
            at = half * half_rows + c * fam_rows + oth * group_rows + i * tokens
            at = pl.ds(pl.multiple_of(at, tokens), tokens)
            sib_at = pl.ds(pl.multiple_of(oth * group_rows + i * tokens, tokens), tokens)
            rest = pl.ds(pl.multiple_of(i * tokens, tokens), tokens)
            total = terms[at, cols].astype(f32) + from_sib[half, sib_at, cols].astype(f32)
            for ref in others:
                total += ref[rest, cols].astype(f32)
            terms[at, cols] = total.astype(bf16)
            return carry

        lax.fori_loop(0, 4, add, 0)

    def to_first(half, h):
        arrived(from_sib.at[half, :, part(h)], sib_sems.at[2 * half + h])
        add_group(half, 1 - other, h, [])
        send(
            terms.at[group_at(half, 1 - other), part(h)],
            from_first.at[half, :, part(h)],
            first_sems.at[2 * half + h],
            first,
        )

    def to_second(h):
        arrived(from_first.at[1, :, part(h)], first_sems.at[2 + h])
        add_group(1, other, h, [from_first.at[1]])
        send(
            terms.at[group_at(1, other), part(h)],
            from_second.at[:, part(h)],
            second_sems.at[h],
            second,
        )

    def to_z(h):
        arrived(from_first.at[0, :, part(h)], first_sems.at[h])
        arrived(from_second.at[:, part(h)], second_sems.at[h])
        add_group(0, other, h, [from_first.at[0], from_second])
        for k in range(3):
            send(
                terms.at[at_slot(slot(0, c, other, peer_z[k])), part(h)],
                from_z.at[k, :, part(h)],
                z_sems.at[3 * h + k],
                peers[k],
            )

    def summed(h):
        total = terms[own_rows, part(h)].astype(f32)
        for k in range(3):
            arrived(from_z.at[k, :, part(h)], z_sems.at[3 * h + k])
        for k in range(3):
            total += from_z[k, :, part(h)].astype(f32)
        return total

    def weight_tiles(left, right_start, out, begin, end):
        tile = 512

        def step(i, carry):
            cols = pl.ds(pl.multiple_of(i * tile, tile), tile)
            right = pl.ds(pl.multiple_of(right_start + i * tile, BLOCK), tile)
            out[:, cols] = jnp.dot(
                left[...], rows_buf[:, right], preferred_element_type=f32
            ).astype(bf16)
            return carry

        lax.fori_loop(begin, end, step, 0)

    compute(0)
    transpose(0, hid_buf, hid_t)
    transpose(0, act_buf, act_t)
    for oth in (other, 1 - other):
        for pz in every_z:
            here = slot(1, c, oth, pz)
            rows_arrived(here)
            send_rows(here, here, sib)
    to_first(0, 0)
    to_first(0, 1)
    for oth in (other, 1 - other):
        for pz in every_z:
            rows_arrived(slot(1, 1 - c, oth, pz))
    compute(1)
    tiles = width // 512
    gate_at, up_at = pl.ds(0, share), pl.ds(share, share)
    out_copies = [
        pltpu.make_async_copy(down_out, grad_down_hbm.at[0], local_sems.at[8]),
        pltpu.make_async_copy(stack_out.at[gate_at], grad_gate_hbm.at[0], local_sems.at[9]),
        pltpu.make_async_copy(stack_out.at[up_at], grad_up_hbm.at[0], local_sems.at[10]),
    ]
    transpose(1, hid_buf, hid_t)
    weight_tiles(hid_t, 0, down_out, 0, tiles // 2)
    to_first(1, 0)
    weight_tiles(hid_t, 0, down_out, tiles // 2, tiles)
    out_copies[0].start()
    to_first(1, 1)
    transpose(1, act_buf, act_t)
    weight_tiles(act_t.at[gate_at], width, stack_out.at[gate_at], 0, tiles)
    out_copies[1].start()
    to_second(0)
    weight_tiles(act_t.at[up_at], width, stack_out.at[up_at], 0, tiles // 2)
    to_second(1)
    weight_tiles(act_t.at[up_at], width, stack_out.at[up_at], tiles // 2, tiles)
    out_copies[2].start()
    to_z(0)
    to_z(1)
    total = summed(0)
    grad_in_ref[:, 0 : width // 2] = total.astype(bf16)
    total = summed(1)
    grad_in_ref[:, width // 2 :] = total[:, 0 : width // 2].astype(bf16)
    comb_total = total[:, width // 2 :]
    place_k = lax.broadcasted_iota(jnp.int32, (picks, tokens), 0)
    comb_out = jnp.zeros((picks, tokens), f32)
    for k in range(picks):
        value = jnp.sum(
            jnp.where(lane == ids[k], comb_total, 0.0), axis=1, keepdims=True
        )
        value = jnp.sum(jnp.where(eye, value, 0.0), axis=0, keepdims=True)
        comb_out += jnp.where(place_k == k, value, 0.0)
    comb_ref[...] = comb_out
    for copy, only in sent:
        if only is None:
            copy.wait_send()
        else:
            pl.when(only)(copy.wait_send)
    for copy in out_copies:
        copy.wait()


def fused_body(grad_out, x_codes, x_scales, combine, expert_ids, w_gate, w_up, w_down):
    tokens, picks = expert_ids.shape
    width, share = grad_out.shape[1], w_gate.shape[1]
    experts = w_gate.shape[0] * lax.axis_size("expert")
    lanes = -(-experts // BLOCK) * BLOCK
    bf16, f32 = jnp.bfloat16, jnp.float32
    back = width + lanes
    vmem = pl.BlockSpec(memory_space=pltpu.VMEM)
    hbm = pl.BlockSpec(memory_space=pltpu.HBM)
    dma = pltpu.SemaphoreType.DMA
    outs = pl.pallas_call(
        functools.partial(expert_kernel, tokens, width, share, lanes, picks),
        out_shape=(
            jax.ShapeDtypeStruct(grad_out.shape, bf16),
            jax.ShapeDtypeStruct((picks, tokens), f32),
            jax.ShapeDtypeStruct(w_gate.shape, bf16),
            jax.ShapeDtypeStruct(w_up.shape, bf16),
            jax.ShapeDtypeStruct(w_down.shape, bf16),
        ),
        in_specs=[hbm] * 8,
        out_specs=(vmem, vmem, hbm, hbm, hbm),
        scratch_shapes=[
            pltpu.VMEM(x_codes.shape, bf16),
            pltpu.VMEM(x_scales.shape, bf16),
            pltpu.VMEM((picks, tokens), jnp.int32),
            pltpu.VMEM((picks, tokens), bf16),
            pltpu.VMEM((32 * tokens, 2 * width + lanes), bf16),
            pltpu.VMEM((2 * share, width), bf16),
            pltpu.VMEM((share, width), bf16),
            pltpu.VMEM((16 * tokens, 2 * share), f32),
            pltpu.VMEM((16 * tokens, share), f32),
            pltpu.VMEM((16 * tokens, 2 * share), bf16),
            pltpu.VMEM((16 * tokens, share), bf16),
            pltpu.VMEM((2 * share, 32 * tokens), bf16),
            pltpu.VMEM((share, 32 * tokens), bf16),
            pltpu.VMEM((2 * share, width), bf16),
            pltpu.VMEM((share, width), bf16),
            pltpu.VMEM((32 * tokens, back), bf16),
            pltpu.VMEM((2, 8 * tokens, back), bf16),
            pltpu.VMEM((2, 4 * tokens, back), bf16),
            pltpu.VMEM((4 * tokens, back), bf16),
            pltpu.VMEM((3, tokens, back), bf16),
            dma((64,)),
            dma((32,)),
            dma((4,)),
            dma((4,)),
            dma((2,)),
            dma((6,)),
            dma((11,)),
        ],
        compiler_params=pltpu.CompilerParams(
            collective_id=0, has_side_effects=True, vmem_limit_bytes=56 * 1024 * 1024
        ),
    )(grad_out, x_codes, x_scales, expert_ids.T, combine.T, w_gate, w_up, w_down)
    return (outs[0], outs[1].T) + tuple(outs[2:])


def chosen_body(grad_out, x_codes, x_scales, combine, expert_ids, w_gate, w_up, w_down):
    tokens, picks = expert_ids.shape
    experts = w_gate.shape[0] * lax.axis_size("expert")
    capacity = min(tokens, max(2, 2 * tokens * picks // experts))
    sizes = (lax.axis_size("dp"), lax.axis_size("expert"), w_gate.shape[0])
    chosen = fused_body if capacity == tokens and sizes == (2, 16, 1) else body
    return chosen(grad_out, x_codes, x_scales, combine, expert_ids, w_gate, w_up, w_down)


def solution(mesh):
    in_specs = (
        P(("dp", "expert"), None),
        P(("dp", "expert"), None),
        P(("dp", "expert"), None),
        P(("dp", "expert"), None),
        P(("dp", "expert"), None),
        P("expert", "dp", None),
        P("expert", "dp", None),
        P("expert", "dp", None),
    )
    out_specs = (
        P(("dp", "expert"), None),
        P(("dp", "expert"), None),
        P("expert", "dp", None),
        P("expert", "dp", None),
        P("expert", "dp", None),
    )
    return jax.shard_map(chosen_body, mesh=mesh, in_specs=in_specs, out_specs=out_specs, check_vma=False)
```

```python
import functools

import jax
import jax.numpy as jnp
from jax import lax
from jax.experimental import pallas as pl
from jax.experimental.pallas import tpu as pltpu
from jax.sharding import PartitionSpec as P

BLOCK = 128
MESH = pl.DeviceIdType.MESH


def slot_table(flat_ids, experts, capacity):
    onehot = (flat_ids[:, None] == jnp.arange(experts, dtype=jnp.int32)[None, :]).astype(jnp.int32)
    before = jnp.cumsum(onehot, axis=0) - onehot
    position = jnp.sum(before * onehot, axis=1)
    slot_index = flat_ids * capacity + position
    return jnp.arange(experts * capacity, dtype=jnp.int32)[:, None] == slot_index[None, :]


def token_owner(placed, tokens, picks):
    return jnp.sum(placed.reshape(placed.shape[0], tokens, picks).astype(jnp.int32), axis=2)


def build_rows(grad_out, x_codes, x_scales, combine, expert_ids, experts, capacity):
    tokens, picks = expert_ids.shape
    placed = slot_table(expert_ids.reshape(-1), experts, capacity)
    owner = token_owner(placed, tokens, picks).astype(jnp.bfloat16)
    grad_rows = jnp.dot(owner, grad_out, preferred_element_type=jnp.float32).astype(jnp.bfloat16)
    code_rows = jnp.dot(owner, x_codes, preferred_element_type=jnp.float32).astype(jnp.bfloat16)
    scale_rows = jnp.dot(owner, x_scales, preferred_element_type=jnp.float32).astype(jnp.bfloat16)
    weight_rows = jnp.dot(
        placed.astype(jnp.bfloat16), combine.reshape(-1), preferred_element_type=jnp.float32
    ).astype(jnp.bfloat16)
    return (
        grad_rows.reshape(experts, capacity, -1),
        code_rows.reshape(experts, capacity, -1),
        scale_rows.reshape(experts, capacity, -1),
        weight_rows.reshape(experts, capacity),
    )


def body(grad_out, x_codes, x_scales, combine, expert_ids, w_gate, w_up, w_down):
    tokens, picks = expert_ids.shape
    width = grad_out.shape[1]
    groups = lax.axis_size("dp")
    experts = w_gate.shape[0] * lax.axis_size("expert")
    capacity = min(tokens, max(2, 2 * tokens * picks // experts))
    grad_rows, code_rows, scale_rows, weight_rows = build_rows(
        grad_out, x_codes, x_scales, combine, expert_ids, experts, capacity
    )
    grad_rows, code_rows, scale_rows, weight_rows = (
        lax.all_to_all(grad_rows, "expert", split_axis=0, concat_axis=0, tiled=True),
        lax.all_to_all(code_rows, "expert", split_axis=0, concat_axis=0, tiled=True),
        lax.all_to_all(scale_rows, "expert", split_axis=0, concat_axis=0, tiled=True),
        lax.all_to_all(weight_rows, "expert", split_axis=0, concat_axis=0, tiled=True),
    )
    grad_rows, code_rows, scale_rows, weight_rows = (
        lax.all_gather(grad_rows[None], "dp", axis=0, tiled=True),
        lax.all_gather(code_rows[None], "dp", axis=0, tiled=True),
        lax.all_gather(scale_rows[None], "dp", axis=0, tiled=True),
        lax.all_gather(weight_rows[None], "dp", axis=0, tiled=True),
    )
    rows = groups * experts * capacity
    scale_count = width // BLOCK
    grad_flat = grad_rows.reshape(rows, width)
    x_rows = (
        (
            code_rows.reshape(rows, scale_count, BLOCK).astype(jnp.float32)
            * scale_rows.reshape(rows, scale_count, 1).astype(jnp.float32)
        )
        .reshape(rows, width)
        .astype(jnp.bfloat16)
    )
    weight_flat = weight_rows.reshape(rows).astype(jnp.float32)
    share = w_gate.shape[1]
    stacked_w = jnp.concatenate([w_gate[0], w_up[0]], axis=0)
    down_w = w_down[0]
    both_pre = lax.dot_general(
        x_rows, stacked_w, (((1,), (1,)), ((), ())), preferred_element_type=jnp.float32
    )
    gate_pre = both_pre[:, :share]
    up_pre = both_pre[:, share:]
    sigmoid_gate = jax.nn.sigmoid(gate_pre)
    activated = gate_pre * sigmoid_gate
    hidden = (activated * up_pre).astype(jnp.bfloat16)
    scaled = (weight_flat[:, None] * grad_flat.astype(jnp.float32)).astype(jnp.bfloat16)
    backward = lax.dot_general(
        grad_flat, down_w, (((1,), (1,)), ((), ())), preferred_element_type=jnp.float32
    )
    partial_comb = jnp.sum(backward * hidden.astype(jnp.float32), axis=1)
    grad_hidden = weight_flat[:, None] * backward
    grad_gate_pre = (
        grad_hidden * up_pre * sigmoid_gate * (1.0 + gate_pre * (1.0 - sigmoid_gate))
    ).astype(jnp.bfloat16)
    grad_up_pre = (grad_hidden * activated).astype(jnp.bfloat16)
    grad_both_pre = jnp.concatenate([grad_gate_pre, grad_up_pre], axis=1)
    grad_down = lax.dot_general(
        hidden, scaled, (((0,), (0,)), ((), ())), preferred_element_type=jnp.float32
    ).astype(jnp.bfloat16)
    grad_stacked = lax.dot_general(
        grad_both_pre, x_rows, (((0,), (0,)), ((), ())), preferred_element_type=jnp.float32
    ).astype(jnp.bfloat16)
    grad_gate = grad_stacked[:share]
    grad_up = grad_stacked[share:]
    input_part = jnp.dot(grad_both_pre, stacked_w, preferred_element_type=jnp.float32)
    summed = lax.psum_scatter(
        input_part.reshape(groups, experts, capacity, width).astype(jnp.bfloat16),
        "dp",
        scatter_dimension=0,
        tiled=True,
    ).astype(jnp.float32)
    comb_all = lax.psum(partial_comb, "dp")
    own_terms = lax.dynamic_slice_in_dim(
        comb_all, lax.axis_index("dp") * (experts * capacity), experts * capacity
    )
    back_grad, back_comb = (
        lax.all_to_all(
            summed.reshape(experts, capacity, width).astype(jnp.bfloat16),
            "expert",
            split_axis=0,
            concat_axis=0,
            tiled=True,
        ).astype(jnp.float32),
        lax.all_to_all(
            own_terms.reshape(experts, capacity).astype(jnp.bfloat16),
            "expert",
            split_axis=0,
            concat_axis=0,
            tiled=True,
        ).astype(jnp.float32),
    )
    placed = slot_table(expert_ids.reshape(-1), experts, capacity)
    owner = token_owner(placed, tokens, picks).astype(jnp.float32)
    grad_in = lax.dot_general(
        owner,
        back_grad.reshape(experts * capacity, width),
        (((0,), (0,)), ((), ())),
        precision=lax.Precision.HIGHEST,
    ).astype(jnp.bfloat16)
    grad_combine = lax.dot_general(
        placed.astype(jnp.float32),
        back_comb.reshape(experts * capacity),
        (((0,), (0,)), ((), ())),
        precision=lax.Precision.HIGHEST,
    ).reshape(tokens, picks)
    return (grad_in, grad_combine, grad_gate[None], grad_up[None], grad_down[None])


def expert_kernel(
    tokens,
    width,
    share,
    lanes,
    picks,
    grad_hbm,
    codes_hbm,
    scales_hbm,
    ids_hbm,
    combine_hbm,
    gate_hbm,
    up_hbm,
    down_hbm,
    grad_in_ref,
    comb_ref,
    grad_gate_hbm,
    grad_up_hbm,
    grad_down_hbm,
    codes_ref,
    scales_ref,
    ids_ref,
    combine_ref,
    rows_buf,
    stack_w,
    down_w,
    pre_buf,
    back_buf,
    act_buf,
    hid_buf,
    act_t,
    hid_t,
    stack_out,
    down_out,
    terms,
    from_sib,
    from_first,
    from_second,
    from_z,
    send_sems,
    row_sems,
    sib_sems,
    first_sems,
    second_sems,
    z_sems,
    local_sems,
):
    f32, bf16 = jnp.float32, jnp.bfloat16
    half_rows, fam_rows, group_rows = 16 * tokens, 8 * tokens, 4 * tokens
    x = lax.axis_index("dp")
    place = lax.axis_index("expert")
    z, y, c = place // 4, (place // 2) % 2, place % 2

    def device(dx, dz, dy, dc):
        return (dx, dz * 4 + dy * 2 + dc)

    sib = device(x, z, y, 1 - c)
    first = device(x + (1 - c) * (1 - 2 * x), z, y + c * (1 - 2 * y), c)
    second = device(x + c * (1 - 2 * x), z, y + (1 - c) * (1 - 2 * y), c)
    peer_z = [z + 1 - 2 * (z % 2), z + 2 - 4 * (z // 2), 3 - z]
    peers = [device(x, pz, y, c) for pz in peer_z]
    other = x + c * (y - x)

    in_copies = [
        pltpu.make_async_copy(gate_hbm.at[0], stack_w.at[pl.ds(0, share)], local_sems.at[0]),
        pltpu.make_async_copy(up_hbm.at[0], stack_w.at[pl.ds(share, share)], local_sems.at[1]),
        pltpu.make_async_copy(down_hbm.at[0], down_w, local_sems.at[2]),
    ]
    own = z + 4 * (2 * c + other)
    own_rows = pl.ds(pl.multiple_of(own * tokens, tokens), tokens)
    own_copies = [
        pltpu.make_async_copy(codes_hbm, codes_ref, local_sems.at[3]),
        pltpu.make_async_copy(scales_hbm, scales_ref, local_sems.at[4]),
        pltpu.make_async_copy(ids_hbm, ids_ref, local_sems.at[5]),
        pltpu.make_async_copy(combine_hbm, combine_ref, local_sems.at[7]),
        pltpu.make_async_copy(grad_hbm, rows_buf.at[own_rows, pl.ds(0, width)], local_sems.at[6]),
    ]
    for copy in own_copies + in_copies:
        copy.start()

    barrier = pltpu.get_barrier_semaphore()
    for partner in [sib, first, second] + peers:
        pl.semaphore_signal(barrier, inc=1, device_id=partner, device_id_type=MESH)

    def slot(half, fam, oth, zz):
        return half * 16 + fam * 8 + oth * 4 + zz

    def at_slot(index):
        return pl.ds(pl.multiple_of(index * tokens, tokens), tokens)

    for copy in own_copies:
        copy.wait()
    scales = scales_ref[...].astype(f32)
    for b in range(width // BLOCK):
        cols = slice(b * BLOCK, (b + 1) * BLOCK)
        rows_buf[own_rows, width + b * BLOCK : width + (b + 1) * BLOCK] = (
            codes_ref[:, cols].astype(f32) * scales[:, b : b + 1]
        ).astype(bf16)
    lane = lax.broadcasted_iota(jnp.int32, (tokens, lanes), 1)
    eye = lax.broadcasted_iota(jnp.int32, (tokens, tokens), 0) == lax.broadcasted_iota(
        jnp.int32, (tokens, tokens), 1
    )

    def column(row):
        return jnp.sum(jnp.where(eye, row, jnp.zeros_like(row)), axis=1, keepdims=True)

    combine = combine_ref[...].astype(f32)
    ids = [column(ids_ref[k : k + 1, :]) for k in range(picks)]
    weight_row = jnp.zeros((tokens, lanes), f32)
    for k in range(picks):
        weight_row += jnp.where(lane == ids[k], column(combine[k : k + 1, :]), 0.0)
    rows_buf[own_rows, 2 * width :] = weight_row.astype(bf16)

    pl.semaphore_wait(barrier, 6)

    sent = []

    def send(src, dst, sem, to, only=None):
        copy = pltpu.make_async_remote_copy(
            src_ref=src,
            dst_ref=dst,
            send_sem=send_sems.at[len(sent)],
            recv_sem=sem,
            device_id=to,
            device_id_type=MESH,
        )
        sent.append((copy, only))
        if only is None:
            copy.start()
        else:
            pl.when(only)(copy.start)

    def arrived(ref, sem):
        pltpu.make_async_remote_copy(
            src_ref=ref,
            dst_ref=ref,
            send_sem=send_sems.at[0],
            recv_sem=sem,
            device_id=sib,
            device_id_type=MESH,
        ).wait_recv()

    row_parts = (pl.ds(0, width), pl.ds(width, width + lanes))

    def send_rows(q, src, dst, to, only=None):
        send(
            rows_buf.at[at_slot(src), row_parts[q]],
            rows_buf.at[at_slot(dst), row_parts[q]],
            row_sems.at[q, dst],
            to,
            only,
        )

    def rows_arrived(q, index):
        arrived(rows_buf.at[at_slot(index), row_parts[q]], row_sems.at[q, index])

    middle = (z == 1) | (z == 2)
    near, across = peers[0], peers[2]
    by_arrival = [peer_z[0], 2 - z // 2, 3 - 3 * (z // 2)]
    every_z = [z] + by_arrival
    for q in range(2):
        send_rows(q, own, own, near)
        send_rows(q, own, own, across, middle)
        send_rows(q, own, own, first)
        send_rows(q, own, own + 16, second)
        send_rows(q, own, own, sib)
    for pz, onward in zip(by_arrival, (across, near, near)):
        here = slot(0, c, other, pz)
        for q in range(2):
            rows_arrived(q, here)
            send_rows(q, here, here, onward, middle)
            send_rows(q, here, here, first)
            send_rows(q, here, here + 16, second)
            send_rows(q, here, here, sib)
    for pz in every_z:
        here = slot(0, c, 1 - other, pz)
        for q in range(2):
            rows_arrived(q, here)
            send_rows(q, here, here + 16, second)
            send_rows(q, here, here, sib)
    for oth in (other, 1 - other):
        for pz in every_z:
            for q in range(2):
                rows_arrived(q, slot(0, 1 - c, oth, pz))
    for copy in in_copies:
        copy.wait()

    contract = (((1,), (1,)), ((), ()))
    strip = 2 * tokens
    mine = lax.broadcasted_iota(jnp.int32, (strip, lanes), 1) == place

    parts = ((0, width // 2), (width // 2, width // 2 + lanes))

    def part(h):
        return pl.ds(*parts[h])

    def compute(half):
        base = half * half_rows
        grad_rows = rows_buf[base : base + half_rows, 0:width]
        x_rows = rows_buf[base : base + half_rows, width : 2 * width]
        pre_buf[...] = lax.dot_general(
            x_rows, stack_w[...], contract, preferred_element_type=f32
        )
        back_buf[...] = lax.dot_general(
            grad_rows, down_w[...], contract, preferred_element_type=f32
        )

        def elementwise(i, carry):
            at = pl.ds(pl.multiple_of(i * strip, strip), strip)
            full = pl.ds(pl.multiple_of(base + i * strip, strip), strip)
            weight = jnp.sum(
                jnp.where(mine, rows_buf[full, 2 * width :].astype(f32), 0.0),
                axis=1,
                keepdims=True,
            )
            gate_pre = pre_buf[at, 0:share]
            up_pre = pre_buf[at, share:]
            backward = back_buf[at, :]
            sigmoid_gate = jax.nn.sigmoid(gate_pre)
            activated = gate_pre * sigmoid_gate
            hidden = activated * up_pre
            comb = jnp.sum(backward * hidden, axis=1, keepdims=True)
            grad_hidden = weight * backward
            act_buf[at, 0:share] = (
                grad_hidden * up_pre * sigmoid_gate * (1.0 + gate_pre * (1.0 - sigmoid_gate))
            ).astype(bf16)
            act_buf[at, share:] = (grad_hidden * activated).astype(bf16)
            hid_buf[at, :] = (weight * hidden).astype(bf16)
            terms[full, width:] = jnp.where(mine, comb, 0.0).astype(bf16)
            return carry

        lax.fori_loop(0, half_rows // strip, elementwise, 0)
        tile = 512

        def back_tile(i, carry):
            cols = pl.ds(pl.multiple_of(i * tile, tile), tile)
            terms[base : base + half_rows, cols] = jnp.dot(
                act_buf[...], stack_w[:, cols], preferred_element_type=f32
            ).astype(bf16)
            return carry

        tiles = width // tile
        lax.fori_loop(0, tiles // 2, back_tile, 0)
        to_sib(half, 0)
        lax.fori_loop(tiles // 2, tiles, back_tile, 0)
        to_sib(half, 1)

    def fam_at(half, fam):
        return pl.ds(pl.multiple_of(half * half_rows + fam * fam_rows, fam_rows), fam_rows)

    def group_at(half, oth):
        return pl.ds(
            pl.multiple_of(half * half_rows + c * fam_rows + oth * group_rows, group_rows),
            group_rows,
        )

    def to_sib(half, h):
        send(
            terms.at[fam_at(half, 1 - c), part(h)],
            from_sib.at[half, :, part(h)],
            sib_sems.at[2 * half + h],
            sib,
        )

    def transpose(half, source, target):
        target[:, half * half_rows : (half + 1) * half_rows] = source[...].T

    def add_group(half, oth, h, others):
        cols = part(h)

        def add(i, carry):
            at = half * half_rows + c * fam_rows + oth * group_rows + i * tokens
            at = pl.ds(pl.multiple_of(at, tokens), tokens)
            sib_at = pl.ds(pl.multiple_of(oth * group_rows + i * tokens, tokens), tokens)
            rest = pl.ds(pl.multiple_of(i * tokens, tokens), tokens)
            total = terms[at, cols].astype(f32) + from_sib[half, sib_at, cols].astype(f32)
            for ref in others:
                total += ref[rest, cols].astype(f32)
            terms[at, cols] = total.astype(bf16)
            return carry

        lax.fori_loop(0, 4, add, 0)

    def to_first(half, h):
        arrived(from_sib.at[half, :, part(h)], sib_sems.at[2 * half + h])
        add_group(half, 1 - other, h, [])
        send(
            terms.at[group_at(half, 1 - other), part(h)],
            from_first.at[half, :, part(h)],
            first_sems.at[2 * half + h],
            first,
        )

    def to_second(h):
        arrived(from_first.at[1, :, part(h)], first_sems.at[2 + h])
        add_group(1, other, h, [from_first.at[1]])
        send(
            terms.at[group_at(1, other), part(h)],
            from_second.at[:, part(h)],
            second_sems.at[h],
            second,
        )

    def to_z(h):
        arrived(from_first.at[0, :, part(h)], first_sems.at[h])
        arrived(from_second.at[:, part(h)], second_sems.at[h])
        add_group(0, other, h, [from_first.at[0], from_second])
        for k in range(3):
            send(
                terms.at[at_slot(slot(0, c, other, peer_z[k])), part(h)],
                from_z.at[k, :, part(h)],
                z_sems.at[3 * h + k],
                peers[k],
            )

    def summed(h):
        total = terms[own_rows, part(h)].astype(f32)
        for k in range(3):
            arrived(from_z.at[k, :, part(h)], z_sems.at[3 * h + k])
        for k in range(3):
            total += from_z[k, :, part(h)].astype(f32)
        return total

    def weight_tiles(left, right_start, out, begin, end):
        tile = 512

        def step(i, carry):
            cols = pl.ds(pl.multiple_of(i * tile, tile), tile)
            right = pl.ds(pl.multiple_of(right_start + i * tile, BLOCK), tile)
            out[:, cols] = jnp.dot(
                left[...], rows_buf[:, right], preferred_element_type=f32
            ).astype(bf16)
            return carry

        lax.fori_loop(begin, end, step, 0)

    compute(0)
    transpose(0, hid_buf, hid_t)
    transpose(0, act_buf, act_t)
    for oth in (other, 1 - other):
        for pz in every_z:
            here = slot(1, c, oth, pz)
            for q in range(2):
                rows_arrived(q, here)
                send_rows(q, here, here, sib)
    to_first(0, 0)
    to_first(0, 1)
    for oth in (other, 1 - other):
        for pz in every_z:
            for q in range(2):
                rows_arrived(q, slot(1, 1 - c, oth, pz))
    compute(1)
    tiles = width // 512
    gate_at, up_at = pl.ds(0, share), pl.ds(share, share)
    out_copies = [
        pltpu.make_async_copy(down_out, grad_down_hbm.at[0], local_sems.at[8]),
        pltpu.make_async_copy(stack_out.at[gate_at], grad_gate_hbm.at[0], local_sems.at[9]),
        pltpu.make_async_copy(stack_out.at[up_at], grad_up_hbm.at[0], local_sems.at[10]),
    ]
    transpose(1, hid_buf, hid_t)
    weight_tiles(hid_t, 0, down_out, 0, tiles // 2)
    to_first(1, 0)
    weight_tiles(hid_t, 0, down_out, tiles // 2, tiles)
    out_copies[0].start()
    to_first(1, 1)
    transpose(1, act_buf, act_t)
    weight_tiles(act_t.at[gate_at], width, stack_out.at[gate_at], 0, tiles)
    out_copies[1].start()
    to_second(0)
    weight_tiles(act_t.at[up_at], width, stack_out.at[up_at], 0, tiles // 2)
    to_second(1)
    weight_tiles(act_t.at[up_at], width, stack_out.at[up_at], tiles // 2, tiles)
    out_copies[2].start()
    to_z(0)
    to_z(1)
    total = summed(0)
    grad_in_ref[:, 0 : width // 2] = total.astype(bf16)
    total = summed(1)
    grad_in_ref[:, width // 2 :] = total[:, 0 : width // 2].astype(bf16)
    comb_total = total[:, width // 2 :]
    place_k = lax.broadcasted_iota(jnp.int32, (picks, tokens), 0)
    comb_out = jnp.zeros((picks, tokens), f32)
    for k in range(picks):
        value = jnp.sum(
            jnp.where(lane == ids[k], comb_total, 0.0), axis=1, keepdims=True
        )
        value = jnp.sum(jnp.where(eye, value, 0.0), axis=0, keepdims=True)
        comb_out += jnp.where(place_k == k, value, 0.0)
    comb_ref[...] = comb_out
    for copy, only in sent:
        if only is None:
            copy.wait_send()
        else:
            pl.when(only)(copy.wait_send)
    for copy in out_copies:
        copy.wait()


def deliver_kernel(*refs):
    sems = refs[10]
    copies = [pltpu.make_async_copy(refs[i], refs[5 + i], sems.at[i]) for i in range(5)]
    for copy in copies:
        copy.start()
    for copy in copies:
        copy.wait()


def fused_body(grad_out, x_codes, x_scales, combine, expert_ids, w_gate, w_up, w_down):
    tokens, picks = expert_ids.shape
    width, share = grad_out.shape[1], w_gate.shape[1]
    experts = w_gate.shape[0] * lax.axis_size("expert")
    lanes = -(-experts // BLOCK) * BLOCK
    bf16, f32 = jnp.bfloat16, jnp.float32
    back = width + lanes
    vmem = pl.BlockSpec(memory_space=pltpu.VMEM)
    hbm = pl.BlockSpec(memory_space=pltpu.HBM)
    dma = pltpu.SemaphoreType.DMA
    outs = pl.pallas_call(
        functools.partial(expert_kernel, tokens, width, share, lanes, picks),
        out_shape=(
            jax.ShapeDtypeStruct(grad_out.shape, bf16),
            jax.ShapeDtypeStruct((picks, tokens), f32),
            jax.ShapeDtypeStruct(w_gate.shape, bf16),
            jax.ShapeDtypeStruct(w_up.shape, bf16),
            jax.ShapeDtypeStruct(w_down.shape, bf16),
        ),
        in_specs=[hbm] * 8,
        out_specs=(vmem, vmem, hbm, hbm, hbm),
        scratch_shapes=[
            pltpu.VMEM(x_codes.shape, bf16),
            pltpu.VMEM(x_scales.shape, bf16),
            pltpu.VMEM((picks, tokens), jnp.int32),
            pltpu.VMEM((picks, tokens), bf16),
            pltpu.VMEM((32 * tokens, 2 * width + lanes), bf16),
            pltpu.VMEM((2 * share, width), bf16),
            pltpu.VMEM((share, width), bf16),
            pltpu.VMEM((16 * tokens, 2 * share), f32),
            pltpu.VMEM((16 * tokens, share), f32),
            pltpu.VMEM((16 * tokens, 2 * share), bf16),
            pltpu.VMEM((16 * tokens, share), bf16),
            pltpu.VMEM((2 * share, 32 * tokens), bf16),
            pltpu.VMEM((share, 32 * tokens), bf16),
            pltpu.VMEM((2 * share, width), bf16),
            pltpu.VMEM((share, width), bf16),
            pltpu.VMEM((32 * tokens, back), bf16),
            pltpu.VMEM((2, 8 * tokens, back), bf16),
            pltpu.VMEM((2, 4 * tokens, back), bf16),
            pltpu.VMEM((4 * tokens, back), bf16),
            pltpu.VMEM((3, tokens, back), bf16),
            dma((96,)),
            dma((2, 32)),
            dma((4,)),
            dma((4,)),
            dma((2,)),
            dma((6,)),
            dma((11,)),
        ],
        compiler_params=pltpu.CompilerParams(
            collective_id=0, has_side_effects=True, vmem_limit_bytes=56 * 1024 * 1024
        ),
    )(grad_out, x_codes, x_scales, expert_ids.T, combine.T, w_gate, w_up, w_down)
    outs = pl.pallas_call(
        deliver_kernel,
        out_shape=tuple(jax.ShapeDtypeStruct(out.shape, out.dtype) for out in outs),
        in_specs=[hbm] * 5,
        out_specs=(hbm,) * 5,
        scratch_shapes=[dma((5,))],
        compiler_params=pltpu.CompilerParams(vmem_limit_bytes=56 * 1024 * 1024),
    )(*outs)
    return (outs[0], outs[1].T) + tuple(outs[2:])


def chosen_body(grad_out, x_codes, x_scales, combine, expert_ids, w_gate, w_up, w_down):
    tokens, picks = expert_ids.shape
    experts = w_gate.shape[0] * lax.axis_size("expert")
    capacity = min(tokens, max(2, 2 * tokens * picks // experts))
    sizes = (lax.axis_size("dp"), lax.axis_size("expert"), w_gate.shape[0])
    chosen = fused_body if capacity == tokens and sizes == (2, 16, 1) else body
    return chosen(grad_out, x_codes, x_scales, combine, expert_ids, w_gate, w_up, w_down)


def solution(mesh):
    in_specs = (
        P(("dp", "expert"), None),
        P(("dp", "expert"), None),
        P(("dp", "expert"), None),
        P(("dp", "expert"), None),
        P(("dp", "expert"), None),
        P("expert", "dp", None),
        P("expert", "dp", None),
        P("expert", "dp", None),
    )
    out_specs = (
        P(("dp", "expert"), None),
        P(("dp", "expert"), None),
        P("expert", "dp", None),
        P("expert", "dp", None),
        P("expert", "dp", None),
    )
    return jax.shard_map(chosen_body, mesh=mesh, in_specs=in_specs, out_specs=out_specs, check_vma=False)
```

```python
import functools

import jax
import jax.numpy as jnp
from jax import lax
from jax.experimental import pallas as pl
from jax.experimental.pallas import tpu as pltpu
from jax.sharding import PartitionSpec as P

BLOCK = 128
MESH = pl.DeviceIdType.MESH


def slot_table(flat_ids, experts, capacity):
    onehot = (flat_ids[:, None] == jnp.arange(experts, dtype=jnp.int32)[None, :]).astype(jnp.int32)
    before = jnp.cumsum(onehot, axis=0) - onehot
    position = jnp.sum(before * onehot, axis=1)
    slot_index = flat_ids * capacity + position
    return jnp.arange(experts * capacity, dtype=jnp.int32)[:, None] == slot_index[None, :]


def token_owner(placed, tokens, picks):
    return jnp.sum(placed.reshape(placed.shape[0], tokens, picks).astype(jnp.int32), axis=2)


def build_rows(grad_out, x_codes, x_scales, combine, expert_ids, experts, capacity):
    tokens, picks = expert_ids.shape
    placed = slot_table(expert_ids.reshape(-1), experts, capacity)
    owner = token_owner(placed, tokens, picks).astype(jnp.bfloat16)
    grad_rows = jnp.dot(owner, grad_out, preferred_element_type=jnp.float32).astype(jnp.bfloat16)
    code_rows = jnp.dot(owner, x_codes, preferred_element_type=jnp.float32).astype(jnp.bfloat16)
    scale_rows = jnp.dot(owner, x_scales, preferred_element_type=jnp.float32).astype(jnp.bfloat16)
    weight_rows = jnp.dot(
        placed.astype(jnp.bfloat16), combine.reshape(-1), preferred_element_type=jnp.float32
    ).astype(jnp.bfloat16)
    return (
        grad_rows.reshape(experts, capacity, -1),
        code_rows.reshape(experts, capacity, -1),
        scale_rows.reshape(experts, capacity, -1),
        weight_rows.reshape(experts, capacity),
    )


def body(grad_out, x_codes, x_scales, combine, expert_ids, w_gate, w_up, w_down):
    tokens, picks = expert_ids.shape
    width = grad_out.shape[1]
    groups = lax.axis_size("dp")
    experts = w_gate.shape[0] * lax.axis_size("expert")
    capacity = min(tokens, max(2, 2 * tokens * picks // experts))
    grad_rows, code_rows, scale_rows, weight_rows = build_rows(
        grad_out, x_codes, x_scales, combine, expert_ids, experts, capacity
    )
    grad_rows, code_rows, scale_rows, weight_rows = (
        lax.all_to_all(grad_rows, "expert", split_axis=0, concat_axis=0, tiled=True),
        lax.all_to_all(code_rows, "expert", split_axis=0, concat_axis=0, tiled=True),
        lax.all_to_all(scale_rows, "expert", split_axis=0, concat_axis=0, tiled=True),
        lax.all_to_all(weight_rows, "expert", split_axis=0, concat_axis=0, tiled=True),
    )
    grad_rows, code_rows, scale_rows, weight_rows = (
        lax.all_gather(grad_rows[None], "dp", axis=0, tiled=True),
        lax.all_gather(code_rows[None], "dp", axis=0, tiled=True),
        lax.all_gather(scale_rows[None], "dp", axis=0, tiled=True),
        lax.all_gather(weight_rows[None], "dp", axis=0, tiled=True),
    )
    rows = groups * experts * capacity
    scale_count = width // BLOCK
    grad_flat = grad_rows.reshape(rows, width)
    x_rows = (
        (
            code_rows.reshape(rows, scale_count, BLOCK).astype(jnp.float32)
            * scale_rows.reshape(rows, scale_count, 1).astype(jnp.float32)
        )
        .reshape(rows, width)
        .astype(jnp.bfloat16)
    )
    weight_flat = weight_rows.reshape(rows).astype(jnp.float32)
    share = w_gate.shape[1]
    stacked_w = jnp.concatenate([w_gate[0], w_up[0]], axis=0)
    down_w = w_down[0]
    both_pre = lax.dot_general(
        x_rows, stacked_w, (((1,), (1,)), ((), ())), preferred_element_type=jnp.float32
    )
    gate_pre = both_pre[:, :share]
    up_pre = both_pre[:, share:]
    sigmoid_gate = jax.nn.sigmoid(gate_pre)
    activated = gate_pre * sigmoid_gate
    hidden = (activated * up_pre).astype(jnp.bfloat16)
    scaled = (weight_flat[:, None] * grad_flat.astype(jnp.float32)).astype(jnp.bfloat16)
    backward = lax.dot_general(
        grad_flat, down_w, (((1,), (1,)), ((), ())), preferred_element_type=jnp.float32
    )
    partial_comb = jnp.sum(backward * hidden.astype(jnp.float32), axis=1)
    grad_hidden = weight_flat[:, None] * backward
    grad_gate_pre = (
        grad_hidden * up_pre * sigmoid_gate * (1.0 + gate_pre * (1.0 - sigmoid_gate))
    ).astype(jnp.bfloat16)
    grad_up_pre = (grad_hidden * activated).astype(jnp.bfloat16)
    grad_both_pre = jnp.concatenate([grad_gate_pre, grad_up_pre], axis=1)
    grad_down = lax.dot_general(
        hidden, scaled, (((0,), (0,)), ((), ())), preferred_element_type=jnp.float32
    ).astype(jnp.bfloat16)
    grad_stacked = lax.dot_general(
        grad_both_pre, x_rows, (((0,), (0,)), ((), ())), preferred_element_type=jnp.float32
    ).astype(jnp.bfloat16)
    grad_gate = grad_stacked[:share]
    grad_up = grad_stacked[share:]
    input_part = jnp.dot(grad_both_pre, stacked_w, preferred_element_type=jnp.float32)
    summed = lax.psum_scatter(
        input_part.reshape(groups, experts, capacity, width).astype(jnp.bfloat16),
        "dp",
        scatter_dimension=0,
        tiled=True,
    ).astype(jnp.float32)
    comb_all = lax.psum(partial_comb, "dp")
    own_terms = lax.dynamic_slice_in_dim(
        comb_all, lax.axis_index("dp") * (experts * capacity), experts * capacity
    )
    back_grad, back_comb = (
        lax.all_to_all(
            summed.reshape(experts, capacity, width).astype(jnp.bfloat16),
            "expert",
            split_axis=0,
            concat_axis=0,
            tiled=True,
        ).astype(jnp.float32),
        lax.all_to_all(
            own_terms.reshape(experts, capacity).astype(jnp.bfloat16),
            "expert",
            split_axis=0,
            concat_axis=0,
            tiled=True,
        ).astype(jnp.float32),
    )
    placed = slot_table(expert_ids.reshape(-1), experts, capacity)
    owner = token_owner(placed, tokens, picks).astype(jnp.float32)
    grad_in = lax.dot_general(
        owner,
        back_grad.reshape(experts * capacity, width),
        (((0,), (0,)), ((), ())),
        precision=lax.Precision.HIGHEST,
    ).astype(jnp.bfloat16)
    grad_combine = lax.dot_general(
        placed.astype(jnp.float32),
        back_comb.reshape(experts * capacity),
        (((0,), (0,)), ((), ())),
        precision=lax.Precision.HIGHEST,
    ).reshape(tokens, picks)
    return (grad_in, grad_combine, grad_gate[None], grad_up[None], grad_down[None])


def expert_kernel(
    tokens,
    width,
    share,
    lanes,
    picks,
    grad_hbm,
    codes_hbm,
    scales_hbm,
    ids_hbm,
    combine_hbm,
    gate_hbm,
    up_hbm,
    down_hbm,
    grad_in_ref,
    comb_ref,
    grad_gate_hbm,
    grad_up_hbm,
    grad_down_hbm,
    codes_ref,
    scales_ref,
    ids_ref,
    combine_ref,
    rows_buf,
    stack_w,
    down_w,
    pre_buf,
    back_buf,
    act_buf,
    hid_buf,
    act_t,
    hid_t,
    stack_out,
    down_out,
    stack_acc,
    down_acc,
    terms,
    from_sib,
    from_first,
    from_second,
    from_z,
    send_sems,
    row_sems,
    sib_sems,
    first_sems,
    second_sems,
    z_sems,
    local_sems,
):
    f32, bf16 = jnp.float32, jnp.bfloat16
    half_rows, fam_rows, group_rows = 16 * tokens, 8 * tokens, 4 * tokens
    x = lax.axis_index("dp")
    place = lax.axis_index("expert")
    z, y, c = place // 4, (place // 2) % 2, place % 2

    def device(dx, dz, dy, dc):
        return (dx, dz * 4 + dy * 2 + dc)

    sib = device(x, z, y, 1 - c)
    first = device(x + (1 - c) * (1 - 2 * x), z, y + c * (1 - 2 * y), c)
    second = device(x + c * (1 - 2 * x), z, y + (1 - c) * (1 - 2 * y), c)
    peer_z = [z + 1 - 2 * (z % 2), z + 2 - 4 * (z // 2), 3 - z]
    peers = [device(x, pz, y, c) for pz in peer_z]
    other = x + c * (y - x)

    in_copies = [
        pltpu.make_async_copy(gate_hbm.at[0], stack_w.at[pl.ds(0, share)], local_sems.at[0]),
        pltpu.make_async_copy(up_hbm.at[0], stack_w.at[pl.ds(share, share)], local_sems.at[1]),
        pltpu.make_async_copy(down_hbm.at[0], down_w, local_sems.at[2]),
    ]
    own = z + 4 * (2 * c + other)
    own_rows = pl.ds(pl.multiple_of(own * tokens, tokens), tokens)
    own_copies = [
        pltpu.make_async_copy(codes_hbm, codes_ref, local_sems.at[3]),
        pltpu.make_async_copy(scales_hbm, scales_ref, local_sems.at[4]),
        pltpu.make_async_copy(ids_hbm, ids_ref, local_sems.at[5]),
        pltpu.make_async_copy(combine_hbm, combine_ref, local_sems.at[7]),
        pltpu.make_async_copy(grad_hbm, rows_buf.at[own_rows, pl.ds(0, width)], local_sems.at[6]),
    ]
    for copy in own_copies + in_copies:
        copy.start()

    barrier = pltpu.get_barrier_semaphore()
    for partner in [sib, first, second] + peers:
        pl.semaphore_signal(barrier, inc=1, device_id=partner, device_id_type=MESH)

    def slot(half, fam, oth, zz):
        return half * 16 + fam * 8 + oth * 4 + zz

    def at_slot(index):
        return pl.ds(pl.multiple_of(index * tokens, tokens), tokens)

    for copy in own_copies:
        copy.wait()
    scales = scales_ref[...].astype(f32)
    for b in range(width // BLOCK):
        cols = slice(b * BLOCK, (b + 1) * BLOCK)
        rows_buf[own_rows, width + b * BLOCK : width + (b + 1) * BLOCK] = (
            codes_ref[:, cols].astype(f32) * scales[:, b : b + 1]
        ).astype(bf16)
    lane = lax.broadcasted_iota(jnp.int32, (tokens, lanes), 1)
    eye = lax.broadcasted_iota(jnp.int32, (tokens, tokens), 0) == lax.broadcasted_iota(
        jnp.int32, (tokens, tokens), 1
    )

    def column(row):
        return jnp.sum(jnp.where(eye, row, jnp.zeros_like(row)), axis=1, keepdims=True)

    combine = combine_ref[...].astype(f32)
    ids = [column(ids_ref[k : k + 1, :]) for k in range(picks)]
    weight_row = jnp.zeros((tokens, lanes), f32)
    for k in range(picks):
        weight_row += jnp.where(lane == ids[k], column(combine[k : k + 1, :]), 0.0)
    rows_buf[own_rows, 2 * width :] = weight_row.astype(bf16)

    pl.semaphore_wait(barrier, 6)

    sent = []

    def send(src, dst, sem, to, only=None):
        copy = pltpu.make_async_remote_copy(
            src_ref=src,
            dst_ref=dst,
            send_sem=send_sems.at[len(sent)],
            recv_sem=sem,
            device_id=to,
            device_id_type=MESH,
        )
        sent.append((copy, only))
        if only is None:
            copy.start()
        else:
            pl.when(only)(copy.start)

    def arrived(ref, sem):
        pltpu.make_async_remote_copy(
            src_ref=ref,
            dst_ref=ref,
            send_sem=send_sems.at[0],
            recv_sem=sem,
            device_id=sib,
            device_id_type=MESH,
        ).wait_recv()

    row_parts = (pl.ds(0, width), pl.ds(width, width + lanes))

    def send_rows(q, src, dst, to, only=None):
        send(
            rows_buf.at[at_slot(src), row_parts[q]],
            rows_buf.at[at_slot(dst), row_parts[q]],
            row_sems.at[q, dst],
            to,
            only,
        )

    def rows_arrived(q, index):
        arrived(rows_buf.at[at_slot(index), row_parts[q]], row_sems.at[q, index])

    middle = (z == 1) | (z == 2)
    near, across = peers[0], peers[2]
    by_arrival = [peer_z[0], 2 - z // 2, 3 - 3 * (z // 2)]
    every_z = [z] + by_arrival
    for q in range(2):
        send_rows(q, own, own, near)
        send_rows(q, own, own, across, middle)
        send_rows(q, own, own, first)
        send_rows(q, own, own + 16, second)
        send_rows(q, own, own, sib)
    for pz, onward in zip(by_arrival, (across, near, near)):
        here = slot(0, c, other, pz)
        for q in range(2):
            rows_arrived(q, here)
            send_rows(q, here, here, onward, middle)
            send_rows(q, here, here, first)
            send_rows(q, here, here + 16, second)
            send_rows(q, here, here, sib)
    for pz in every_z:
        here = slot(0, c, 1 - other, pz)
        for q in range(2):
            rows_arrived(q, here)
            send_rows(q, here, here + 16, second)
            send_rows(q, here, here, sib)
    for oth in (other, 1 - other):
        for pz in every_z:
            for q in range(2):
                rows_arrived(q, slot(0, 1 - c, oth, pz))
    for copy in in_copies:
        copy.wait()

    contract = (((1,), (1,)), ((), ()))
    strip = 2 * tokens
    mine = lax.broadcasted_iota(jnp.int32, (strip, lanes), 1) == place

    parts = ((0, width // 2), (width // 2, width // 2 + lanes))

    def part(h):
        return pl.ds(*parts[h])

    def compute(half):
        base = half * half_rows
        grad_rows = rows_buf[base : base + half_rows, 0:width]
        x_rows = rows_buf[base : base + half_rows, width : 2 * width]
        pre_buf[...] = lax.dot_general(
            x_rows, stack_w[...], contract, preferred_element_type=f32
        )
        back_buf[...] = lax.dot_general(
            grad_rows, down_w[...], contract, preferred_element_type=f32
        )

        def elementwise(i, carry):
            at = pl.ds(pl.multiple_of(i * strip, strip), strip)
            full = pl.ds(pl.multiple_of(base + i * strip, strip), strip)
            weight = jnp.sum(
                jnp.where(mine, rows_buf[full, 2 * width :].astype(f32), 0.0),
                axis=1,
                keepdims=True,
            )
            gate_pre = pre_buf[at, 0:share]
            up_pre = pre_buf[at, share:]
            backward = back_buf[at, :]
            sigmoid_gate = jax.nn.sigmoid(gate_pre)
            activated = gate_pre * sigmoid_gate
            hidden = activated * up_pre
            comb = jnp.sum(backward * hidden, axis=1, keepdims=True)
            grad_hidden = weight * backward
            act_buf[at, 0:share] = (
                grad_hidden * up_pre * sigmoid_gate * (1.0 + gate_pre * (1.0 - sigmoid_gate))
            ).astype(bf16)
            act_buf[at, share:] = (grad_hidden * activated).astype(bf16)
            hid_buf[at, :] = (weight * hidden).astype(bf16)
            terms[full, width:] = jnp.where(mine, comb, 0.0).astype(bf16)
            return carry

        lax.fori_loop(0, half_rows // strip, elementwise, 0)
        tile = 512

        def back_tile(i, carry):
            cols = pl.ds(pl.multiple_of(i * tile, tile), tile)
            terms[base : base + half_rows, cols] = jnp.dot(
                act_buf[...], stack_w[:, cols], preferred_element_type=f32
            ).astype(bf16)
            return carry

        tiles = width // tile
        lax.fori_loop(0, tiles // 2, back_tile, 0)
        to_sib(half, 0)
        lax.fori_loop(tiles // 2, tiles, back_tile, 0)
        to_sib(half, 1)

    def fam_at(half, fam):
        return pl.ds(pl.multiple_of(half * half_rows + fam * fam_rows, fam_rows), fam_rows)

    def group_at(half, oth):
        return pl.ds(
            pl.multiple_of(half * half_rows + c * fam_rows + oth * group_rows, group_rows),
            group_rows,
        )

    def to_sib(half, h):
        send(
            terms.at[fam_at(half, 1 - c), part(h)],
            from_sib.at[half, :, part(h)],
            sib_sems.at[2 * half + h],
            sib,
        )

    def transpose(half, source, target):
        target[:, half * half_rows : (half + 1) * half_rows] = source[...].T

    def add_group(half, oth, h, others):
        cols = part(h)

        def add(i, carry):
            at = half * half_rows + c * fam_rows + oth * group_rows + i * tokens
            at = pl.ds(pl.multiple_of(at, tokens), tokens)
            sib_at = pl.ds(pl.multiple_of(oth * group_rows + i * tokens, tokens), tokens)
            rest = pl.ds(pl.multiple_of(i * tokens, tokens), tokens)
            total = terms[at, cols].astype(f32) + from_sib[half, sib_at, cols].astype(f32)
            for ref in others:
                total += ref[rest, cols].astype(f32)
            terms[at, cols] = total.astype(bf16)
            return carry

        lax.fori_loop(0, 4, add, 0)

    def to_first(half, h):
        arrived(from_sib.at[half, :, part(h)], sib_sems.at[2 * half + h])
        add_group(half, 1 - other, h, [])
        send(
            terms.at[group_at(half, 1 - other), part(h)],
            from_first.at[half, :, part(h)],
            first_sems.at[2 * half + h],
            first,
        )

    def to_second(h):
        arrived(from_first.at[1, :, part(h)], first_sems.at[2 + h])
        add_group(1, other, h, [from_first.at[1]])
        send(
            terms.at[group_at(1, other), part(h)],
            from_second.at[:, part(h)],
            second_sems.at[h],
            second,
        )

    def to_z(h):
        arrived(from_first.at[0, :, part(h)], first_sems.at[h])
        arrived(from_second.at[:, part(h)], second_sems.at[h])
        add_group(0, other, h, [from_first.at[0], from_second])
        for k in range(3):
            send(
                terms.at[at_slot(slot(0, c, other, peer_z[k])), part(h)],
                from_z.at[k, :, part(h)],
                z_sems.at[3 * h + k],
                peers[k],
            )

    def summed(h):
        total = terms[own_rows, part(h)].astype(f32)
        for k in range(3):
            arrived(from_z.at[k, :, part(h)], z_sems.at[3 * h + k])
        for k in range(3):
            total += from_z[k, :, part(h)].astype(f32)
        return total

    def weight_tiles(half, left, right_start, acc, out, begin, end):
        tile = 512
        taken = slice(half * half_rows, (half + 1) * half_rows)

        def step(i, carry):
            cols = pl.ds(pl.multiple_of(i * tile, tile), tile)
            right = pl.ds(pl.multiple_of(right_start + i * tile, BLOCK), tile)
            product = jnp.dot(left[:, taken], rows_buf[taken, right], preferred_element_type=f32)
            if half == 0:
                acc[:, cols] = product
            else:
                out[:, cols] = (acc[:, cols] + product).astype(bf16)
            return carry

        lax.fori_loop(begin, end, step, 0)

    tiles = width // 512
    gate_at, up_at = pl.ds(0, share), pl.ds(share, share)

    def down_tiles(half, begin, end):
        weight_tiles(half, hid_t, 0, down_acc, down_out, begin, end)

    def stack_tiles(half, at, begin, end):
        weight_tiles(
            half, act_t.at[at], width, stack_acc.at[at], stack_out.at[at], begin, end
        )

    compute(0)
    transpose(0, hid_buf, hid_t)
    transpose(0, act_buf, act_t)
    to_first(0, 0)
    to_first(0, 1)

    def pass_on(oth):
        for pz in every_z:
            here = slot(1, c, oth, pz)
            for q in range(2):
                rows_arrived(q, here)
                send_rows(q, here, here, sib)

    down_tiles(0, 0, tiles)
    pass_on(other)
    stack_tiles(0, gate_at, 0, tiles)
    stack_tiles(0, up_at, 0, tiles)
    pass_on(1 - other)
    for oth in (other, 1 - other):
        for pz in every_z:
            for q in range(2):
                rows_arrived(q, slot(1, 1 - c, oth, pz))
    compute(1)
    out_copies = [
        pltpu.make_async_copy(down_out, grad_down_hbm.at[0], local_sems.at[8]),
        pltpu.make_async_copy(stack_out.at[gate_at], grad_gate_hbm.at[0], local_sems.at[9]),
        pltpu.make_async_copy(stack_out.at[up_at], grad_up_hbm.at[0], local_sems.at[10]),
    ]
    transpose(1, hid_buf, hid_t)
    down_tiles(1, 0, tiles // 2)
    to_first(1, 0)
    down_tiles(1, tiles // 2, tiles)
    out_copies[0].start()
    to_first(1, 1)
    transpose(1, act_buf, act_t)
    stack_tiles(1, gate_at, 0, tiles)
    out_copies[1].start()
    to_second(0)
    stack_tiles(1, up_at, 0, tiles // 2)
    to_second(1)
    stack_tiles(1, up_at, tiles // 2, tiles)
    out_copies[2].start()
    to_z(0)
    to_z(1)
    total = summed(0)
    grad_in_ref[:, 0 : width // 2] = total.astype(bf16)
    total = summed(1)
    grad_in_ref[:, width // 2 :] = total[:, 0 : width // 2].astype(bf16)
    comb_total = total[:, width // 2 :]
    place_k = lax.broadcasted_iota(jnp.int32, (picks, tokens), 0)
    comb_out = jnp.zeros((picks, tokens), f32)
    for k in range(picks):
        value = jnp.sum(
            jnp.where(lane == ids[k], comb_total, 0.0), axis=1, keepdims=True
        )
        value = jnp.sum(jnp.where(eye, value, 0.0), axis=0, keepdims=True)
        comb_out += jnp.where(place_k == k, value, 0.0)
    comb_ref[...] = comb_out
    for copy, only in sent:
        if only is None:
            copy.wait_send()
        else:
            pl.when(only)(copy.wait_send)
    for copy in out_copies:
        copy.wait()


def deliver_kernel(*refs):
    sources, results, held, sems = refs[:5], refs[5:10], refs[10:15], refs[15]
    pieces = []
    for i in range(5):
        if len(sources[i].shape) == 3:
            step = sources[i].shape[1] // 4
            for j in range(4):
                at = pl.ds(j * step, step)
                pieces.append((sources[i].at[0, at], held[i].at[0, at], results[i].at[0, at]))
        else:
            pieces.append((sources[i], held[i], results[i]))
    reads = [
        pltpu.make_async_copy(piece[0], piece[1], sems.at[0, n]) for n, piece in enumerate(pieces)
    ]
    writes = [
        pltpu.make_async_copy(piece[1], piece[2], sems.at[1, n]) for n, piece in enumerate(pieces)
    ]
    for copy in reads:
        copy.start()
    for n in range(len(pieces)):
        reads[n].wait()
        writes[n].start()
    for copy in writes:
        copy.wait()


def fused_body(grad_out, x_codes, x_scales, combine, expert_ids, w_gate, w_up, w_down):
    tokens, picks = expert_ids.shape
    width, share = grad_out.shape[1], w_gate.shape[1]
    experts = w_gate.shape[0] * lax.axis_size("expert")
    lanes = -(-experts // BLOCK) * BLOCK
    bf16, f32 = jnp.bfloat16, jnp.float32
    back = width + lanes
    vmem = pl.BlockSpec(memory_space=pltpu.VMEM)
    hbm = pl.BlockSpec(memory_space=pltpu.HBM)
    dma = pltpu.SemaphoreType.DMA
    outs = pl.pallas_call(
        functools.partial(expert_kernel, tokens, width, share, lanes, picks),
        out_shape=(
            jax.ShapeDtypeStruct(grad_out.shape, bf16),
            jax.ShapeDtypeStruct((picks, tokens), f32),
            jax.ShapeDtypeStruct(w_gate.shape, bf16),
            jax.ShapeDtypeStruct(w_up.shape, bf16),
            jax.ShapeDtypeStruct(w_down.shape, bf16),
        ),
        in_specs=[hbm] * 8,
        out_specs=(vmem, vmem, hbm, hbm, hbm),
        scratch_shapes=[
            pltpu.VMEM(x_codes.shape, bf16),
            pltpu.VMEM(x_scales.shape, bf16),
            pltpu.VMEM((picks, tokens), jnp.int32),
            pltpu.VMEM((picks, tokens), bf16),
            pltpu.VMEM((32 * tokens, 2 * width + lanes), bf16),
            pltpu.VMEM((2 * share, width), bf16),
            pltpu.VMEM((share, width), bf16),
            pltpu.VMEM((16 * tokens, 2 * share), f32),
            pltpu.VMEM((16 * tokens, share), f32),
            pltpu.VMEM((16 * tokens, 2 * share), bf16),
            pltpu.VMEM((16 * tokens, share), bf16),
            pltpu.VMEM((2 * share, 32 * tokens), bf16),
            pltpu.VMEM((share, 32 * tokens), bf16),
            pltpu.VMEM((2 * share, width), bf16),
            pltpu.VMEM((share, width), bf16),
            pltpu.VMEM((2 * share, width), f32),
            pltpu.VMEM((share, width), f32),
            pltpu.VMEM((32 * tokens, back), bf16),
            pltpu.VMEM((2, 8 * tokens, back), bf16),
            pltpu.VMEM((2, 4 * tokens, back), bf16),
            pltpu.VMEM((4 * tokens, back), bf16),
            pltpu.VMEM((3, tokens, back), bf16),
            dma((96,)),
            dma((2, 32)),
            dma((4,)),
            dma((4,)),
            dma((2,)),
            dma((6,)),
            dma((11,)),
        ],
        compiler_params=pltpu.CompilerParams(
            collective_id=0, has_side_effects=True, vmem_limit_bytes=56 * 1024 * 1024
        ),
    )(grad_out, x_codes, x_scales, expert_ids.T, combine.T, w_gate, w_up, w_down)
    outs = pl.pallas_call(
        deliver_kernel,
        out_shape=tuple(jax.ShapeDtypeStruct(out.shape, out.dtype) for out in outs),
        in_specs=[hbm] * 5,
        out_specs=(hbm,) * 5,
        scratch_shapes=[pltpu.VMEM(out.shape, out.dtype) for out in outs] + [dma((2, 14))],
        compiler_params=pltpu.CompilerParams(vmem_limit_bytes=56 * 1024 * 1024),
    )(*outs)
    return (outs[0], outs[1].T) + tuple(outs[2:])


def chosen_body(grad_out, x_codes, x_scales, combine, expert_ids, w_gate, w_up, w_down):
    tokens, picks = expert_ids.shape
    experts = w_gate.shape[0] * lax.axis_size("expert")
    capacity = min(tokens, max(2, 2 * tokens * picks // experts))
    sizes = (lax.axis_size("dp"), lax.axis_size("expert"), w_gate.shape[0])
    chosen = fused_body if capacity == tokens and sizes == (2, 16, 1) else body
    return chosen(grad_out, x_codes, x_scales, combine, expert_ids, w_gate, w_up, w_down)


def solution(mesh):
    in_specs = (
        P(("dp", "expert"), None),
        P(("dp", "expert"), None),
        P(("dp", "expert"), None),
        P(("dp", "expert"), None),
        P(("dp", "expert"), None),
        P("expert", "dp", None),
        P("expert", "dp", None),
        P("expert", "dp", None),
    )
    out_specs = (
        P(("dp", "expert"), None),
        P(("dp", "expert"), None),
        P("expert", "dp", None),
        P("expert", "dp", None),
        P("expert", "dp", None),
    )
    return jax.shard_map(chosen_body, mesh=mesh, in_specs=in_specs, out_specs=out_specs, check_vma=False)
```

```python
import functools

import jax
import jax.numpy as jnp
from jax import lax
from jax.experimental import pallas as pl
from jax.experimental.pallas import tpu as pltpu
from jax.sharding import PartitionSpec as P

BLOCK = 128
MESH = pl.DeviceIdType.MESH


def slot_table(flat_ids, experts, capacity):
    onehot = (flat_ids[:, None] == jnp.arange(experts, dtype=jnp.int32)[None, :]).astype(jnp.int32)
    before = jnp.cumsum(onehot, axis=0) - onehot
    position = jnp.sum(before * onehot, axis=1)
    slot_index = flat_ids * capacity + position
    return jnp.arange(experts * capacity, dtype=jnp.int32)[:, None] == slot_index[None, :]


def token_owner(placed, tokens, picks):
    return jnp.sum(placed.reshape(placed.shape[0], tokens, picks).astype(jnp.int32), axis=2)


def build_rows(grad_out, x_codes, x_scales, combine, expert_ids, experts, capacity):
    tokens, picks = expert_ids.shape
    placed = slot_table(expert_ids.reshape(-1), experts, capacity)
    owner = token_owner(placed, tokens, picks).astype(jnp.bfloat16)
    grad_rows = jnp.dot(owner, grad_out, preferred_element_type=jnp.float32).astype(jnp.bfloat16)
    code_rows = jnp.dot(owner, x_codes, preferred_element_type=jnp.float32).astype(jnp.bfloat16)
    scale_rows = jnp.dot(owner, x_scales, preferred_element_type=jnp.float32).astype(jnp.bfloat16)
    weight_rows = jnp.dot(
        placed.astype(jnp.bfloat16), combine.reshape(-1), preferred_element_type=jnp.float32
    ).astype(jnp.bfloat16)
    return (
        grad_rows.reshape(experts, capacity, -1),
        code_rows.reshape(experts, capacity, -1),
        scale_rows.reshape(experts, capacity, -1),
        weight_rows.reshape(experts, capacity),
    )


def body(grad_out, x_codes, x_scales, combine, expert_ids, w_gate, w_up, w_down):
    tokens, picks = expert_ids.shape
    width = grad_out.shape[1]
    groups = lax.axis_size("dp")
    experts = w_gate.shape[0] * lax.axis_size("expert")
    capacity = min(tokens, max(2, 2 * tokens * picks // experts))
    grad_rows, code_rows, scale_rows, weight_rows = build_rows(
        grad_out, x_codes, x_scales, combine, expert_ids, experts, capacity
    )
    grad_rows, code_rows, scale_rows, weight_rows = (
        lax.all_to_all(grad_rows, "expert", split_axis=0, concat_axis=0, tiled=True),
        lax.all_to_all(code_rows, "expert", split_axis=0, concat_axis=0, tiled=True),
        lax.all_to_all(scale_rows, "expert", split_axis=0, concat_axis=0, tiled=True),
        lax.all_to_all(weight_rows, "expert", split_axis=0, concat_axis=0, tiled=True),
    )
    grad_rows, code_rows, scale_rows, weight_rows = (
        lax.all_gather(grad_rows[None], "dp", axis=0, tiled=True),
        lax.all_gather(code_rows[None], "dp", axis=0, tiled=True),
        lax.all_gather(scale_rows[None], "dp", axis=0, tiled=True),
        lax.all_gather(weight_rows[None], "dp", axis=0, tiled=True),
    )
    rows = groups * experts * capacity
    scale_count = width // BLOCK
    grad_flat = grad_rows.reshape(rows, width)
    x_rows = (
        (
            code_rows.reshape(rows, scale_count, BLOCK).astype(jnp.float32)
            * scale_rows.reshape(rows, scale_count, 1).astype(jnp.float32)
        )
        .reshape(rows, width)
        .astype(jnp.bfloat16)
    )
    weight_flat = weight_rows.reshape(rows).astype(jnp.float32)
    share = w_gate.shape[1]
    stacked_w = jnp.concatenate([w_gate[0], w_up[0]], axis=0)
    down_w = w_down[0]
    both_pre = lax.dot_general(
        x_rows, stacked_w, (((1,), (1,)), ((), ())), preferred_element_type=jnp.float32
    )
    gate_pre = both_pre[:, :share]
    up_pre = both_pre[:, share:]
    sigmoid_gate = jax.nn.sigmoid(gate_pre)
    activated = gate_pre * sigmoid_gate
    hidden = (activated * up_pre).astype(jnp.bfloat16)
    scaled = (weight_flat[:, None] * grad_flat.astype(jnp.float32)).astype(jnp.bfloat16)
    backward = lax.dot_general(
        grad_flat, down_w, (((1,), (1,)), ((), ())), preferred_element_type=jnp.float32
    )
    partial_comb = jnp.sum(backward * hidden.astype(jnp.float32), axis=1)
    grad_hidden = weight_flat[:, None] * backward
    grad_gate_pre = (
        grad_hidden * up_pre * sigmoid_gate * (1.0 + gate_pre * (1.0 - sigmoid_gate))
    ).astype(jnp.bfloat16)
    grad_up_pre = (grad_hidden * activated).astype(jnp.bfloat16)
    grad_both_pre = jnp.concatenate([grad_gate_pre, grad_up_pre], axis=1)
    grad_down = lax.dot_general(
        hidden, scaled, (((0,), (0,)), ((), ())), preferred_element_type=jnp.float32
    ).astype(jnp.bfloat16)
    grad_stacked = lax.dot_general(
        grad_both_pre, x_rows, (((0,), (0,)), ((), ())), preferred_element_type=jnp.float32
    ).astype(jnp.bfloat16)
    grad_gate = grad_stacked[:share]
    grad_up = grad_stacked[share:]
    input_part = jnp.dot(grad_both_pre, stacked_w, preferred_element_type=jnp.float32)
    summed = lax.psum_scatter(
        input_part.reshape(groups, experts, capacity, width).astype(jnp.bfloat16),
        "dp",
        scatter_dimension=0,
        tiled=True,
    ).astype(jnp.float32)
    comb_all = lax.psum(partial_comb, "dp")
    own_terms = lax.dynamic_slice_in_dim(
        comb_all, lax.axis_index("dp") * (experts * capacity), experts * capacity
    )
    back_grad, back_comb = (
        lax.all_to_all(
            summed.reshape(experts, capacity, width).astype(jnp.bfloat16),
            "expert",
            split_axis=0,
            concat_axis=0,
            tiled=True,
        ).astype(jnp.float32),
        lax.all_to_all(
            own_terms.reshape(experts, capacity).astype(jnp.bfloat16),
            "expert",
            split_axis=0,
            concat_axis=0,
            tiled=True,
        ).astype(jnp.float32),
    )
    placed = slot_table(expert_ids.reshape(-1), experts, capacity)
    owner = token_owner(placed, tokens, picks).astype(jnp.float32)
    grad_in = lax.dot_general(
        owner,
        back_grad.reshape(experts * capacity, width),
        (((0,), (0,)), ((), ())),
        precision=lax.Precision.HIGHEST,
    ).astype(jnp.bfloat16)
    grad_combine = lax.dot_general(
        placed.astype(jnp.float32),
        back_comb.reshape(experts * capacity),
        (((0,), (0,)), ((), ())),
        precision=lax.Precision.HIGHEST,
    ).reshape(tokens, picks)
    return (grad_in, grad_combine, grad_gate[None], grad_up[None], grad_down[None])


def expert_kernel(
    tokens,
    width,
    share,
    lanes,
    picks,
    grad_hbm,
    codes_hbm,
    scales_hbm,
    ids_hbm,
    combine_hbm,
    gate_hbm,
    up_hbm,
    down_hbm,
    grad_in_ref,
    comb_ref,
    grad_gate_hbm,
    grad_up_hbm,
    grad_down_hbm,
    codes_ref,
    scales_ref,
    ids_ref,
    combine_ref,
    rows_buf,
    stack_w,
    down_w,
    pre_buf,
    back_buf,
    act_buf,
    hid_buf,
    act_t,
    hid_t,
    stack_out,
    down_out,
    terms,
    from_sib,
    from_first,
    from_second,
    from_z,
    send_sems,
    row_sems,
    sib_sems,
    first_sems,
    second_sems,
    z_sems,
    local_sems,
):
    f32, bf16 = jnp.float32, jnp.bfloat16
    half_rows, fam_rows, group_rows = 16 * tokens, 8 * tokens, 4 * tokens
    x = lax.axis_index("dp")
    place = lax.axis_index("expert")
    z, y, c = place // 4, (place // 2) % 2, place % 2

    def device(dx, dz, dy, dc):
        return (dx, dz * 4 + dy * 2 + dc)

    sib = device(x, z, y, 1 - c)
    first = device(x + (1 - c) * (1 - 2 * x), z, y + c * (1 - 2 * y), c)
    second = device(x + c * (1 - 2 * x), z, y + (1 - c) * (1 - 2 * y), c)
    peer_z = [z + 1 - 2 * (z % 2), z + 2 - 4 * (z // 2), 3 - z]
    peers = [device(x, pz, y, c) for pz in peer_z]
    other = x + c * (y - x)

    in_copies = [
        pltpu.make_async_copy(gate_hbm.at[0], stack_w.at[pl.ds(0, share)], local_sems.at[0]),
        pltpu.make_async_copy(up_hbm.at[0], stack_w.at[pl.ds(share, share)], local_sems.at[1]),
        pltpu.make_async_copy(down_hbm.at[0], down_w, local_sems.at[2]),
    ]
    own = z + 4 * (2 * c + other)
    own_rows = pl.ds(pl.multiple_of(own * tokens, tokens), tokens)
    own_copies = [
        pltpu.make_async_copy(codes_hbm, codes_ref, local_sems.at[3]),
        pltpu.make_async_copy(scales_hbm, scales_ref, local_sems.at[4]),
        pltpu.make_async_copy(ids_hbm, ids_ref, local_sems.at[5]),
        pltpu.make_async_copy(combine_hbm, combine_ref, local_sems.at[7]),
        pltpu.make_async_copy(grad_hbm, rows_buf.at[own_rows, pl.ds(0, width)], local_sems.at[6]),
    ]
    for copy in own_copies + in_copies:
        copy.start()

    barrier = pltpu.get_barrier_semaphore()
    for partner in [sib, first, second] + peers:
        pl.semaphore_signal(barrier, inc=1, device_id=partner, device_id_type=MESH)

    def slot(half, fam, oth, zz):
        return half * 16 + fam * 8 + oth * 4 + zz

    def at_slot(index):
        return pl.ds(pl.multiple_of(index * tokens, tokens), tokens)

    for copy in own_copies:
        copy.wait()
    scales = scales_ref[...].astype(f32)
    for b in range(width // BLOCK):
        cols = slice(b * BLOCK, (b + 1) * BLOCK)
        rows_buf[own_rows, width + b * BLOCK : width + (b + 1) * BLOCK] = (
            codes_ref[:, cols].astype(f32) * scales[:, b : b + 1]
        ).astype(bf16)
    lane = lax.broadcasted_iota(jnp.int32, (tokens, lanes), 1)
    eye = lax.broadcasted_iota(jnp.int32, (tokens, tokens), 0) == lax.broadcasted_iota(
        jnp.int32, (tokens, tokens), 1
    )

    def column(row):
        return jnp.sum(jnp.where(eye, row, jnp.zeros_like(row)), axis=1, keepdims=True)

    combine = combine_ref[...].astype(f32)
    ids = [column(ids_ref[k : k + 1, :]) for k in range(picks)]
    weight_row = jnp.zeros((tokens, lanes), f32)
    for k in range(picks):
        weight_row += jnp.where(lane == ids[k], column(combine[k : k + 1, :]), 0.0)
    rows_buf[own_rows, 2 * width :] = weight_row.astype(bf16)

    pl.semaphore_wait(barrier, 6)

    sent = []

    def send(src, dst, sem, to, only=None):
        copy = pltpu.make_async_remote_copy(
            src_ref=src,
            dst_ref=dst,
            send_sem=send_sems.at[len(sent)],
            recv_sem=sem,
            device_id=to,
            device_id_type=MESH,
        )
        sent.append((copy, only))
        if only is None:
            copy.start()
        else:
            pl.when(only)(copy.start)

    def arrived(ref, sem):
        pltpu.make_async_remote_copy(
            src_ref=ref,
            dst_ref=ref,
            send_sem=send_sems.at[0],
            recv_sem=sem,
            device_id=sib,
            device_id_type=MESH,
        ).wait_recv()

    row_parts = (pl.ds(0, width), pl.ds(width, width + lanes))

    def send_rows(q, src, dst, to, only=None):
        send(
            rows_buf.at[at_slot(src), row_parts[q]],
            rows_buf.at[at_slot(dst), row_parts[q]],
            row_sems.at[q, dst],
            to,
            only,
        )

    def rows_arrived(q, index):
        arrived(rows_buf.at[at_slot(index), row_parts[q]], row_sems.at[q, index])

    middle = (z == 1) | (z == 2)
    near, across = peers[0], peers[2]
    by_arrival = [peer_z[0], 2 - z // 2, 3 - 3 * (z // 2)]
    every_z = [z] + by_arrival
    for q in range(2):
        send_rows(q, own, own, near)
        send_rows(q, own, own, across, middle)
        send_rows(q, own, own, first)
        send_rows(q, own, own + 16, second)
        send_rows(q, own, own, sib)
    for pz, onward in zip(by_arrival, (across, near, near)):
        here = slot(0, c, other, pz)
        for q in range(2):
            rows_arrived(q, here)
            send_rows(q, here, here, onward, middle)
            send_rows(q, here, here, first)
            send_rows(q, here, here + 16, second)
            send_rows(q, here, here, sib)
    for pz in every_z:
        here = slot(0, c, 1 - other, pz)
        for q in range(2):
            rows_arrived(q, here)
            send_rows(q, here, here + 16, second)
            send_rows(q, here, here, sib)
    for oth in (other, 1 - other):
        for pz in every_z:
            for q in range(2):
                rows_arrived(q, slot(0, 1 - c, oth, pz))
    for copy in in_copies:
        copy.wait()

    contract = (((1,), (1,)), ((), ()))
    strip = 2 * tokens
    mine = lax.broadcasted_iota(jnp.int32, (strip, lanes), 1) == place

    parts = ((0, width // 2), (width // 2, width // 2 + lanes))

    def part(h):
        return pl.ds(*parts[h])

    def compute(half):
        base = half * half_rows
        grad_rows = rows_buf[base : base + half_rows, 0:width]
        x_rows = rows_buf[base : base + half_rows, width : 2 * width]
        pre_buf[...] = lax.dot_general(
            x_rows, stack_w[...], contract, preferred_element_type=f32
        )
        back_buf[...] = lax.dot_general(
            grad_rows, down_w[...], contract, preferred_element_type=f32
        )

        def elementwise(i, carry):
            at = pl.ds(pl.multiple_of(i * strip, strip), strip)
            full = pl.ds(pl.multiple_of(base + i * strip, strip), strip)
            weight = jnp.sum(
                jnp.where(mine, rows_buf[full, 2 * width :].astype(f32), 0.0),
                axis=1,
                keepdims=True,
            )
            gate_pre = pre_buf[at, 0:share]
            up_pre = pre_buf[at, share:]
            backward = back_buf[at, :]
            sigmoid_gate = jax.nn.sigmoid(gate_pre)
            activated = gate_pre * sigmoid_gate
            hidden = activated * up_pre
            comb = jnp.sum(backward * hidden, axis=1, keepdims=True)
            grad_hidden = weight * backward
            act_buf[at, 0:share] = (
                grad_hidden * up_pre * sigmoid_gate * (1.0 + gate_pre * (1.0 - sigmoid_gate))
            ).astype(bf16)
            act_buf[at, share:] = (grad_hidden * activated).astype(bf16)
            hid_buf[at, :] = (weight * hidden).astype(bf16)
            terms[full, width:] = jnp.where(mine, comb, 0.0).astype(bf16)
            return carry

        lax.fori_loop(0, half_rows // strip, elementwise, 0)
        tile = 512

        def back_tile(i, carry):
            cols = pl.ds(pl.multiple_of(i * tile, tile), tile)
            terms[base : base + half_rows, cols] = jnp.dot(
                act_buf[...], stack_w[:, cols], preferred_element_type=f32
            ).astype(bf16)
            return carry

        tiles = width // tile
        lax.fori_loop(0, tiles // 2, back_tile, 0)
        to_sib(half, 0)
        lax.fori_loop(tiles // 2, tiles, back_tile, 0)
        to_sib(half, 1)

    def fam_at(half, fam):
        return pl.ds(pl.multiple_of(half * half_rows + fam * fam_rows, fam_rows), fam_rows)

    def group_at(half, oth):
        return pl.ds(
            pl.multiple_of(half * half_rows + c * fam_rows + oth * group_rows, group_rows),
            group_rows,
        )

    def to_sib(half, h):
        send(
            terms.at[fam_at(half, 1 - c), part(h)],
            from_sib.at[half, :, part(h)],
            sib_sems.at[2 * half + h],
            sib,
        )

    def transpose(half, source, target):
        target[:, half * half_rows : (half + 1) * half_rows] = source[...].T

    def add_group(half, oth, h, others):
        cols = part(h)

        def add(i, carry):
            at = half * half_rows + c * fam_rows + oth * group_rows + i * tokens
            at = pl.ds(pl.multiple_of(at, tokens), tokens)
            sib_at = pl.ds(pl.multiple_of(oth * group_rows + i * tokens, tokens), tokens)
            rest = pl.ds(pl.multiple_of(i * tokens, tokens), tokens)
            total = terms[at, cols].astype(f32) + from_sib[half, sib_at, cols].astype(f32)
            for ref in others:
                total += ref[rest, cols].astype(f32)
            terms[at, cols] = total.astype(bf16)
            return carry

        lax.fori_loop(0, 4, add, 0)

    def to_first(half, h):
        arrived(from_sib.at[half, :, part(h)], sib_sems.at[2 * half + h])
        add_group(half, 1 - other, h, [])
        send(
            terms.at[group_at(half, 1 - other), part(h)],
            from_first.at[half, :, part(h)],
            first_sems.at[2 * half + h],
            first,
        )

    def to_second(h):
        arrived(from_first.at[1, :, part(h)], first_sems.at[2 + h])
        add_group(1, other, h, [from_first.at[1]])
        send(
            terms.at[group_at(1, other), part(h)],
            from_second.at[:, part(h)],
            second_sems.at[h],
            second,
        )

    def to_z(h):
        arrived(from_first.at[0, :, part(h)], first_sems.at[h])
        arrived(from_second.at[:, part(h)], second_sems.at[h])
        add_group(0, other, h, [from_first.at[0], from_second])
        for k in range(3):
            send(
                terms.at[at_slot(slot(0, c, other, peer_z[k])), part(h)],
                from_z.at[k, :, part(h)],
                z_sems.at[3 * h + k],
                peers[k],
            )

    def summed(h):
        total = terms[own_rows, part(h)].astype(f32)
        for k in range(3):
            arrived(from_z.at[k, :, part(h)], z_sems.at[3 * h + k])
        for k in range(3):
            total += from_z[k, :, part(h)].astype(f32)
        return total

    def weight_tiles(left, right_start, out, begin, end):
        tile = 512

        def step(i, carry):
            cols = pl.ds(pl.multiple_of(i * tile, tile), tile)
            right = pl.ds(pl.multiple_of(right_start + i * tile, BLOCK), tile)
            out[:, cols] = jnp.dot(
                left[...], rows_buf[:, right], preferred_element_type=f32
            ).astype(bf16)
            return carry

        lax.fori_loop(begin, end, step, 0)

    compute(0)
    transpose(0, hid_buf, hid_t)
    transpose(0, act_buf, act_t)
    for oth in (other, 1 - other):
        for pz in every_z:
            here = slot(1, c, oth, pz)
            for q in range(2):
                rows_arrived(q, here)
                send_rows(q, here, here, sib)
    to_first(0, 0)
    to_first(0, 1)
    for oth in (other, 1 - other):
        for pz in every_z:
            for q in range(2):
                rows_arrived(q, slot(1, 1 - c, oth, pz))
    compute(1)
    tiles = width // 512
    gate_at, up_at = pl.ds(0, share), pl.ds(share, share)
    out_copies = [
        pltpu.make_async_copy(down_out, grad_down_hbm.at[0], local_sems.at[8]),
        pltpu.make_async_copy(stack_out.at[gate_at], grad_gate_hbm.at[0], local_sems.at[9]),
        pltpu.make_async_copy(stack_out.at[up_at], grad_up_hbm.at[0], local_sems.at[10]),
    ]
    transpose(1, hid_buf, hid_t)
    weight_tiles(hid_t, 0, down_out, 0, tiles // 2)
    to_first(1, 0)
    weight_tiles(hid_t, 0, down_out, tiles // 2, tiles)
    out_copies[0].start()
    to_first(1, 1)
    transpose(1, act_buf, act_t)
    weight_tiles(act_t.at[gate_at], width, stack_out.at[gate_at], 0, tiles)
    out_copies[1].start()
    to_second(0)
    weight_tiles(act_t.at[up_at], width, stack_out.at[up_at], 0, tiles // 2)
    to_second(1)
    weight_tiles(act_t.at[up_at], width, stack_out.at[up_at], tiles // 2, tiles)
    out_copies[2].start()
    to_z(0)
    to_z(1)
    total = summed(0)
    grad_in_ref[:, 0 : width // 2] = total.astype(bf16)
    total = summed(1)
    grad_in_ref[:, width // 2 :] = total[:, 0 : width // 2].astype(bf16)
    comb_total = total[:, width // 2 :]
    place_k = lax.broadcasted_iota(jnp.int32, (picks, tokens), 0)
    comb_out = jnp.zeros((picks, tokens), f32)
    for k in range(picks):
        value = jnp.sum(
            jnp.where(lane == ids[k], comb_total, 0.0), axis=1, keepdims=True
        )
        value = jnp.sum(jnp.where(eye, value, 0.0), axis=0, keepdims=True)
        comb_out += jnp.where(place_k == k, value, 0.0)
    comb_ref[...] = comb_out
    for copy, only in sent:
        if only is None:
            copy.wait_send()
        else:
            pl.when(only)(copy.wait_send)
    for copy in out_copies:
        copy.wait()


def deliver_kernel(*refs):
    sources, results, held, sems = refs[:5], refs[5:10], refs[10:15], refs[15]
    pieces = []
    for i in range(5):
        if len(sources[i].shape) == 3:
            step = sources[i].shape[1] // 4
            for j in range(4):
                at = pl.ds(j * step, step)
                pieces.append((sources[i].at[0, at], held[i].at[0, at], results[i].at[0, at]))
        else:
            pieces.append((sources[i], held[i], results[i]))
    reads = [
        pltpu.make_async_copy(piece[0], piece[1], sems.at[0, n]) for n, piece in enumerate(pieces)
    ]
    writes = [
        pltpu.make_async_copy(piece[1], piece[2], sems.at[1, n]) for n, piece in enumerate(pieces)
    ]
    for copy in reads:
        copy.start()
    for n in range(len(pieces)):
        reads[n].wait()
        writes[n].start()
    for copy in writes:
        copy.wait()


def fused_body(grad_out, x_codes, x_scales, combine, expert_ids, w_gate, w_up, w_down):
    tokens, picks = expert_ids.shape
    width, share = grad_out.shape[1], w_gate.shape[1]
    experts = w_gate.shape[0] * lax.axis_size("expert")
    lanes = -(-experts // BLOCK) * BLOCK
    bf16, f32 = jnp.bfloat16, jnp.float32
    back = width + lanes
    vmem = pl.BlockSpec(memory_space=pltpu.VMEM)
    hbm = pl.BlockSpec(memory_space=pltpu.HBM)
    dma = pltpu.SemaphoreType.DMA
    outs = pl.pallas_call(
        functools.partial(expert_kernel, tokens, width, share, lanes, picks),
        out_shape=(
            jax.ShapeDtypeStruct(grad_out.shape, bf16),
            jax.ShapeDtypeStruct((picks, tokens), f32),
            jax.ShapeDtypeStruct(w_gate.shape, bf16),
            jax.ShapeDtypeStruct(w_up.shape, bf16),
            jax.ShapeDtypeStruct(w_down.shape, bf16),
        ),
        in_specs=[hbm] * 8,
        out_specs=(vmem, vmem, hbm, hbm, hbm),
        scratch_shapes=[
            pltpu.VMEM(x_codes.shape, bf16),
            pltpu.VMEM(x_scales.shape, bf16),
            pltpu.VMEM((picks, tokens), jnp.int32),
            pltpu.VMEM((picks, tokens), bf16),
            pltpu.VMEM((32 * tokens, 2 * width + lanes), bf16),
            pltpu.VMEM((2 * share, width), bf16),
            pltpu.VMEM((share, width), bf16),
            pltpu.VMEM((16 * tokens, 2 * share), f32),
            pltpu.VMEM((16 * tokens, share), f32),
            pltpu.VMEM((16 * tokens, 2 * share), bf16),
            pltpu.VMEM((16 * tokens, share), bf16),
            pltpu.VMEM((2 * share, 32 * tokens), bf16),
            pltpu.VMEM((share, 32 * tokens), bf16),
            pltpu.VMEM((2 * share, width), bf16),
            pltpu.VMEM((share, width), bf16),
            pltpu.VMEM((32 * tokens, back), bf16),
            pltpu.VMEM((2, 8 * tokens, back), bf16),
            pltpu.VMEM((2, 4 * tokens, back), bf16),
            pltpu.VMEM((4 * tokens, back), bf16),
            pltpu.VMEM((3, tokens, back), bf16),
            dma((96,)),
            dma((2, 32)),
            dma((4,)),
            dma((4,)),
            dma((2,)),
            dma((6,)),
            dma((11,)),
        ],
        compiler_params=pltpu.CompilerParams(
            collective_id=0, has_side_effects=True, vmem_limit_bytes=56 * 1024 * 1024
        ),
    )(grad_out, x_codes, x_scales, expert_ids.T, combine.T, w_gate, w_up, w_down)
    outs = pl.pallas_call(
        deliver_kernel,
        out_shape=tuple(jax.ShapeDtypeStruct(out.shape, out.dtype) for out in outs),
        in_specs=[hbm] * 5,
        out_specs=(hbm,) * 5,
        scratch_shapes=[pltpu.VMEM(out.shape, out.dtype) for out in outs] + [dma((2, 14))],
        compiler_params=pltpu.CompilerParams(vmem_limit_bytes=56 * 1024 * 1024),
    )(*outs)
    return (outs[0], outs[1].T) + tuple(outs[2:])


def chosen_body(grad_out, x_codes, x_scales, combine, expert_ids, w_gate, w_up, w_down):
    tokens, picks = expert_ids.shape
    experts = w_gate.shape[0] * lax.axis_size("expert")
    capacity = min(tokens, max(2, 2 * tokens * picks // experts))
    sizes = (lax.axis_size("dp"), lax.axis_size("expert"), w_gate.shape[0])
    chosen = fused_body if capacity == tokens and sizes == (2, 16, 1) else body
    return chosen(grad_out, x_codes, x_scales, combine, expert_ids, w_gate, w_up, w_down)


def solution(mesh):
    in_specs = (
        P(("dp", "expert"), None),
        P(("dp", "expert"), None),
        P(("dp", "expert"), None),
        P(("dp", "expert"), None),
        P(("dp", "expert"), None),
        P("expert", "dp", None),
        P("expert", "dp", None),
        P("expert", "dp", None),
    )
    out_specs = (
        P(("dp", "expert"), None),
        P(("dp", "expert"), None),
        P("expert", "dp", None),
        P("expert", "dp", None),
        P("expert", "dp", None),
    )
    return jax.shard_map(chosen_body, mesh=mesh, in_specs=in_specs, out_specs=out_specs, check_vma=False)
```
